128 devices in a mesh: ctx: 32 (over x, y, core), row: 4 (over z).
Axes of the slice: x: 4, y: 4, z: 4, core: 2. Of those that a mesh axis runs over, the one named last changes fastest.
Arguments:
- queries: bfloat16 [32, 2, 384, 1024], P('ctx', None, 'row'), may hold values from -110 to 110
- keys: bfloat16 [32, 2, 384, 128], P('ctx', None, 'row'), may hold values from -5 to 5
- values: bfloat16 [32, 2, 384, 128], P('ctx', None, 'row'), may hold values from -6 to 6
- assignment: int32 [32, 2], replicated, may hold values from 0 to 63, as said below
Outputs:
- attended: bfloat16 [32, 2, 384, 1024], P('ctx', None, 'row')
- log_total: float32 [32, 2, 8, 384], P('ctx', None, None, 'row')
The draws below stay inside these ranges and needn't reach their ends.
Inputs may be any that keep to these rules, and one draw needn't show every extreme that they name: Every span number 0 to 63 stands exactly once in assignment.
All inputs are finite; a program needn't handle non-finite values.
Results may differ from the reference program's by a relative error of at most 0.017.
Values may be sent and summed in bfloat16 or wider, within the bound.
No kernel may reach another device: no remote copies, remote signals or barrier semaphores. Data moves between devices by JAX's collectives and lax.ppermute only.
A program may use at most 64 MiB of HBM per device.

```python
import jax
import jax.numpy as jnp
from jax import lax

H = 8
HD = 128
SPAN = 384
N_CTX = 32


def shared_keys(key):
    return jnp.clip(jax.random.normal(key, (N_CTX, 2, SPAN, HD), jnp.float32), -5.0, 5.0)


def draw_keys(key, part):
    shared = shared_keys(key)
    return shared.astype(jnp.bfloat16)


def draw_queries(key, part):
    key = jax.random.fold_in(key, 5)
    drawn = 2.5 * jax.random.normal(key, (N_CTX, 2, SPAN, H, HD), jnp.float32)
    return jnp.clip(drawn, -15.0, 15.0).reshape(N_CTX, 2, SPAN, H * HD).astype(jnp.bfloat16)


def draw_assignment(key, part):
    key = jax.random.fold_in(key, 7)
    return jax.random.permutation(key, 2 * N_CTX).astype(jnp.int32).reshape(N_CTX, 2)


def level_of(rng, dims, pieces, least, top_value):
    loudness, own = 1.0, jax.random.fold_in(rng, 6)
    for dim, blocks in pieces:
        steps = jnp.exp(jax.random.uniform(jax.random.fold_in(own, dim), (blocks,), jnp.float32, least / len(pieces), top_value / len(pieces)))
        loudness = loudness * jnp.repeat(steps, dims[dim] // blocks).reshape([-1 if axis == dim else 1 for axis in range(len(dims))])
    return loudness


def centred(stream_key, shape, width, reach, cuts=(), kind=jnp.bfloat16):
    gain = level_of(stream_key, shape, cuts, -0.22, 0.18) if cuts else 1.0
    array = jax.random.normal(stream_key, shape, jnp.float32) * width * gain
    return jnp.minimum(jnp.maximum(array, -reach), reach).astype(kind)


def setup_inputs(seed: int = 0) -> dict:
    seeds = jax.random.split(jax.random.key(seed), 5)
    queries = draw_queries(jax.random.fold_in(seeds[4], 71), 0)
    keys = draw_keys(jax.random.fold_in(seeds[4], 71), 0)
    values = centred(seeds[2], (N_CTX, 2, SPAN, HD), 1.0, 6.0, ((0, 32), (2, 4)))
    assignment = draw_assignment(jax.random.fold_in(seeds[4], 71), 0)
    return dict(queries=queries, keys=keys, values=values, assignment=assignment)


def reference(queries, keys, values, assignment):
    score_scale = 1.0 / (HD ** 0.5)
    key_pos = (assignment[:, :, None] * SPAN + jnp.arange(SPAN, dtype=jnp.int32)[None, None, :]).reshape(-1).astype(jnp.int32)
    key_rows = keys.reshape(-1, HD).astype(jnp.float32)
    value_rows = values.reshape(-1, HD).astype(jnp.float32)
    query_all = queries.reshape(N_CTX * 2, SPAN, H, HD)
    query_pos_all = key_pos.reshape(N_CTX * 2, SPAN)

    def one_span(inputs):
        query_blk, query_pos = inputs
        scores = jnp.einsum("thd,sd->hts", query_blk.astype(jnp.float32), key_rows) * score_scale
        allowed = key_pos[None, None, :] <= query_pos[None, :, None]
        scores = jnp.where(allowed, scores, -1e30)
        row_max = jnp.max(scores, axis=-1)
        weights = jnp.where(allowed, jnp.exp(scores - row_max[..., None]), 0.0)
        row_sum = jnp.sum(weights, axis=-1)
        rounded = lax.optimization_barrier(weights.astype(jnp.bfloat16))
        summed = jnp.einsum("hts,sd->thd", rounded.astype(jnp.float32), value_rows)
        attended = (summed / jnp.transpose(row_sum)[:, :, None]).astype(jnp.bfloat16)
        return attended.reshape(SPAN, H * HD), row_max + jnp.log(row_sum)

    attended, log_total = lax.map(one_span, (query_all, query_pos_all))
    return attended.reshape(N_CTX, 2, SPAN, H * HD), log_total.reshape(N_CTX, 2, H, SPAN)
```

```python
import functools

import jax
import jax.numpy as jnp
from jax import lax
from jax.experimental import pallas as pl
from jax.experimental.pallas import tpu as pltpu
from jax.sharding import PartitionSpec as P

BF, F32, I32 = jnp.bfloat16, jnp.float32, jnp.int32
NX, NY, NC, NZ = 4, 4, 2, 4
HEADS, HD, SPAN = 8, 128, 384
ROWS = SPAN // NZ
HALF = ROWS // 2
TQ = HEADS * ROWS
NK = NY * NC * 2
MAX_STEPS = 8 * NK // 2
NEG = -1e30
SCALE = 1.4426950408889634 / HD**0.5
LN2 = 0.6931471805599453


def shift_x(a, d):
    perm = [
        ((x * NY + y) * NC + c, ((x + d) % NX * NY + y) * NC + c)
        for x in range(NX) for y in range(NY) for c in range(NC)
    ]
    return lax.ppermute(a, "ctx", perm)


def shift_y(a, d):
    perm = [
        ((x * NY + y) * NC + c, (x * NY + (y + d) % NY) * NC + c)
        for x in range(NX) for y in range(NY) for c in range(NC)
    ]
    return lax.ppermute(a, "ctx", perm)


def shift_z(a, d):
    return lax.ppermute(a, "row", [(z, (z + d) % NZ) for z in range(NZ)])


def swap_core(a):
    return lax.ppermute(a, "ctx", [(i, i ^ 1) for i in range(NX * NY * NC)])


def dot(a, b):
    return lax.dot_general(a, b, (((1,), (0,)), ((), ())), preferred_element_type=F32)


REL = (0, -1, 1, 2)


def gather_two(a, first, second):
    low, high = first(a, 1), first(a, -1)
    far = jnp.stack([first(low[0], 1), first(high[1], -1)])
    line = jnp.stack([a, low, high, far], axis=1)
    low, high = second(line, 1), second(line, -1)
    return line, low, high, second(low[0], 1), second(high[1], -1)


def arrange_kernel(at_ref, *refs):
    inputs, (out_ref, vals) = refs[:10], refs[10:]
    here = {"y": at_ref[0], "z": at_ref[1]}
    for piece, (one, two) in enumerate((("y", "z"), ("z", "y"))):
        line, low, high, far_k, far_v = inputs[5 * piece : 5 * piece + 5]
        for i, di in enumerate(REL):
            for j, dj in enumerate(REL):
                place = {one: lax.rem(here[one] + di + 4, 4), two: lax.rem(here[two] + dj + 4, 4)}
                for slot in range(2):
                    if j < 3:
                        src = (line, low, high)[j]
                        k, v = src[0, i, slot], src[1, i, slot]
                    else:
                        k, v = far_k[i, slot], far_v[i, slot]
                    span = place["y"] * 2 + slot
                    at = pl.multiple_of(place["z"] * ROWS + piece * HALF, 16)
                    out_ref[span, pl.ds(at, HALF), :] = k
                    vals[span, pl.ds(at, HALF), :] = v

    def turn(span, _):
        for b in range(3):
            block = vals[span, b * 128 : (b + 1) * 128, :]
            out_ref[span, SPAN + b * 128 : SPAN + (b + 1) * 128, :] = block.astype(F32).T.astype(BF)
        return 0

    lax.fori_loop(0, 2 * NY, turn, 0)


def arrange(at, pieces):
    vmem = pl.BlockSpec(memory_space=pltpu.VMEM)
    return pl.pallas_call(
        arrange_kernel,
        out_shape=jax.ShapeDtypeStruct((2 * NY, 2 * SPAN, HD), BF),
        in_specs=[pl.BlockSpec(memory_space=pltpu.SMEM)] + [vmem] * 10,
        out_specs=vmem,
        scratch_shapes=[pltpu.VMEM((2 * NY, SPAN, HD), BF)],
        compiler_params=pltpu.CompilerParams(vmem_limit_bytes=40 << 20),
        name="arrange",
    )(at, *pieces)


def attend_kernel(q0, groups, diagonal, table, *refs):
    nq = 2 * groups
    queries, (kv_own, kv_other) = refs[:groups], refs[groups : groups + 2]
    outs, lses = refs[groups + 2 : 2 * groups + 2], refs[2 * groups + 2 : 3 * groups + 2]
    kv, qt, s0, s1, p0, p1, t0, t1, acc, o_buf, l_buf, sems = refs[3 * groups + 2 :]
    copies = [
        pltpu.make_async_copy(kv_own, kv.at[: NK // 2], sems.at[0]),
        pltpu.make_async_copy(kv_other, kv.at[NK // 2 :], sems.at[1]),
    ]
    for c in copies:
        c.start()
    for g in range(groups):
        for slot in range(2):
            full = queries[g][0, slot].astype(F32) * SCALE
            rows = jnp.concatenate([full[:, h * HD : (h + 1) * HD] for h in range(HEADS)], axis=0)
            turned = rows.T
            high = turned.astype(BF)
            qt[2 * g + slot, :HD, :] = high
            qt[2 * g + slot, HD:, :] = (turned - high.astype(F32)).astype(BF)
    o_buf[...] = jnp.zeros_like(o_buf)
    l_buf[...] = jnp.full_like(l_buf, NEG)
    acc[...] = jnp.zeros_like(acc)
    p1[...] = jnp.zeros_like(p1)
    base = table[6, q0]
    steps = table[6, q0 + nq] - base
    for c in copies:
        c.wait()

    def entry(row, i):
        return table[row, base + jnp.clip(i, 0, jnp.maximum(steps - 1, 0))]

    def tile_of(i):
        return jnp.clip(entry(0, i) - q0, 0, nq - 1)

    def flag(row, i):
        return jnp.logical_and(jnp.logical_and(i >= 0, i < steps), entry(row, i) == 1)

    def score(i, s, t):
        q = qt[tile_of(i)]
        for half in range(2):
            k = kv[entry(1 + half, i), :SPAN, :]
            x = dot(jnp.concatenate([k, k], axis=1), q)
            s[half * SPAN : (half + 1) * SPAN, :] = x
            t[half : half + 1, :] = jnp.max(x, axis=0, keepdims=True)

    def mask(i, s, t):
        row = table[6, 9]
        for half in range(2):
            @pl.when(jnp.logical_and(flag(4, i), (entry(5, i) == 1) == (half == 0)))
            def _():
                block = s[half * SPAN : (half + 1) * SPAN, :]
                key = lax.broadcasted_iota(I32, (SPAN, TQ), 0)
                query = lax.rem(lax.broadcasted_iota(I32, (SPAN, TQ), 1), ROWS) + row * ROWS
                block = jnp.where(key <= query, block, NEG)
                s[half * SPAN : (half + 1) * SPAN, :] = block
                t[half : half + 1, :] = jnp.max(block, axis=0, keepdims=True)

    def softmax(i, s, t, p, m, l):
        first, pad = flag(3, i), flag(5, i)
        m = jnp.where(first, NEG, m)
        last_half = jnp.where(pad, NEG, t[1:2, :])
        new = jnp.maximum(jnp.maximum(m, t[0:1, :]), last_half)
        rescale = jnp.exp2(m - new)
        total = jnp.zeros_like(l)
        for half in range(2):
            top = new if half == 0 else jnp.where(pad, -NEG, new)
            w = jnp.exp2(s[half * SPAN : (half + 1) * SPAN, :] - top)
            total += jnp.sum(w, axis=0, keepdims=True)
            p[half * SPAN : (half + 1) * SPAN, :] = w.astype(BF)
        return new, l * rescale + total, rescale

    def weigh(i, p, rescale):
        v = []
        for half in range(2):
            k = entry(1 + half, i)
            v += [kv[k, SPAN + b * HD : SPAN + (b + 1) * HD, :] for b in range(3)]
        acc[...] = acc[...] * rescale + dot(jnp.concatenate(v, axis=1), p[...])

    def finish(i, m, l):
        @pl.when(flag(4, i))
        def _():
            t = tile_of(i)
            o_buf[t] = (acc[...] / l).T.astype(BF)
            l_buf[t] = m * LN2 + jnp.log(l)

    def step(i, s_in, s_out, t_in, t_out, p_in, p_out, carry):
        m, l, rescale = carry
        if diagonal:
            mask(i, s_in, t_in)
        new = softmax(i, s_in, t_in, p_out, m, l)
        weigh(i - 1, p_in, rescale)
        score(i + 1, s_out, t_out)
        finish(i - 1, m, l)
        return new

    def pair(ii, carry):
        i = 2 * ii
        carry = step(i, s0, s1, t0, t1, p1, p0, carry)
        return step(i + 1, s1, s0, t1, t0, p0, p1, carry)

    row = jnp.zeros((1, TQ), F32)
    score(0, s0, t0)
    lax.fori_loop(0, (steps + 2) // 2, pair, (row + NEG, row, row + 1.0))
    for g in range(groups):
        for slot in range(2):
            for h in range(HEADS):
                outs[g][0, slot, :, h * HD : (h + 1) * HD] = o_buf[2 * g + slot, h * ROWS : (h + 1) * ROWS, :]
                lses[g][slot, h : h + 1, :] = l_buf[2 * g + slot][:, h * ROWS : (h + 1) * ROWS]


def attend(q0, diagonal, table, queries, kv_own, kv_other):
    groups = len(queries)
    vmem = pl.BlockSpec(memory_space=pltpu.VMEM)
    hbm = pl.BlockSpec(memory_space=pl.ANY)
    tile = 2 * SPAN
    flops = 2 * 2 * groups * TQ * NK * SPAN * HD * 2 // 2
    results = pl.pallas_call(
        functools.partial(attend_kernel, q0, groups, diagonal),
        out_shape=[jax.ShapeDtypeStruct((1, 2, ROWS, HEADS * HD), BF)] * groups
        + [jax.ShapeDtypeStruct((2, HEADS, ROWS), F32)] * groups,
        in_specs=[pl.BlockSpec(memory_space=pltpu.SMEM)] + [vmem] * groups + [hbm] * 2,
        out_specs=[vmem] * (2 * groups),
        scratch_shapes=[
            pltpu.VMEM((NK, 2 * SPAN, HD), BF),
            pltpu.VMEM((2 * groups, 2 * HD, TQ), BF),
            pltpu.VMEM((tile, TQ), F32),
            pltpu.VMEM((tile, TQ), F32),
            pltpu.VMEM((tile, TQ), BF),
            pltpu.VMEM((tile, TQ), BF),
            pltpu.VMEM((8, TQ), F32),
            pltpu.VMEM((8, TQ), F32),
            pltpu.VMEM((HD, TQ), F32),
            pltpu.VMEM((2 * groups, TQ, HD), BF),
            pltpu.VMEM((2 * groups, 1, TQ), F32),
            pltpu.SemaphoreType.DMA((2,)),
        ],
        compiler_params=pltpu.CompilerParams(vmem_limit_bytes=48 << 20),
        cost_estimate=pl.CostEstimate(flops=flops, bytes_accessed=6 << 20, transcendentals=flops // 512),
        name="attend",
    )(table, *queries, kv_own, kv_other)
    return results[:groups], results[groups:]


def combine_kernel(*refs):
    parts, lses, (out_ref, lse_ref) = refs[:4], refs[4:8], refs[8:]
    for slot in range(2):
        logs = [r[slot] for r in lses]
        top = functools.reduce(jnp.maximum, logs)
        raw = [jnp.exp(v - top) for v in logs]
        total = sum(raw)
        lse_ref[0, slot] = top + jnp.log(total)
        shares = [(r / total).T for r in raw]
        for h in range(HEADS):
            cols = slice(h * HD, (h + 1) * HD)
            mixed = sum(s[:, h : h + 1] * r[0, slot, :, cols].astype(F32) for s, r in zip(shares, parts))
            out_ref[0, slot, :, cols] = mixed.astype(BF)


def combine(parts, lses):
    vmem = pl.BlockSpec(memory_space=pltpu.VMEM)
    return pl.pallas_call(
        combine_kernel,
        out_shape=(
            jax.ShapeDtypeStruct((1, 2, ROWS, HEADS * HD), BF),
            jax.ShapeDtypeStruct((1, 2, HEADS, ROWS), F32),
        ),
        in_specs=[vmem] * 8,
        out_specs=(vmem, vmem),
        compiler_params=pltpu.CompilerParams(vmem_limit_bytes=32 << 20),
        name="combine",
    )(*parts, *lses)


def step_table(assignment, x, y, core, row):
    spans = assignment.reshape(NX, NY, NC, 2)
    plane = lax.dynamic_index_in_dim(spans, x, 0, keepdims=False)
    own = lax.dynamic_index_in_dim(plane, core, 1, keepdims=False).reshape(-1)
    other = lax.dynamic_index_in_dim(plane, 1 - core, 1, keepdims=False).reshape(-1)
    keys = jnp.concatenate([own, other])
    column = lax.dynamic_slice(spans, (0, y, core, 0), (NX, 1, 1, 2)).reshape(NX, 2)
    query = jnp.concatenate(
        [lax.dynamic_index_in_dim(column, (x + d) % NX, 0, keepdims=False) for d in (2, -1, 1, 0)]
    )
    index = jnp.arange(NK, dtype=I32)
    rank = jnp.sum((keys[None, :] < keys[:, None]).astype(I32), axis=1)
    count = jnp.sum((keys[None, :] <= query[:, None]).astype(I32), axis=1)
    tiles = (count + 1) // 2
    before = jnp.tril(jnp.ones((9, 8), I32), -1)
    start = jnp.sum(before * tiles[None, :], axis=1)
    step = jnp.arange(MAX_STEPS, dtype=I32)
    tile = jnp.minimum(jnp.sum((start[None, 1:] <= step[:, None]).astype(I32), axis=1), 7)
    hot = (tile[:, None] == jnp.arange(8, dtype=I32)[None, :]).astype(I32)
    pick = lambda v: jnp.sum(hot * v[None, :], axis=1)
    j = step - pick(start[:8])

    def at_rank(r):
        return jnp.sum(jnp.where(rank[None, :] == jnp.clip(r, 0, NK - 1)[:, None], index[None, :], 0), axis=1)

    last = (j == pick(tiles) - 1).astype(I32)
    odd = last * (pick(count) % 2)
    meta = jnp.zeros((MAX_STEPS,), I32).at[:9].set(start).at[9].set(row)
    first = (j == 0).astype(I32)
    return jnp.stack([tile, at_rank(2 * j), at_rank(2 * j + 1), first, last, odd, meta, meta])


def local(queries, keys, values, assignment):
    ctx, row = lax.axis_index("ctx"), lax.axis_index("row")
    x, y, core = ctx // (NY * NC), ctx // NC % NY, ctx % NC
    kv = jnp.stack([keys[0], values[0]])
    pieces = gather_two(kv[:, :, :HALF], shift_y, shift_z) + gather_two(kv[:, :, HALF:], shift_z, shift_y)
    from_low, from_high = shift_x(queries, 1), shift_x(queries, -1)
    far = jnp.stack([shift_x(from_low[:, 0], 1), shift_x(from_high[:, 1], -1)], axis=1)
    table = step_table(assignment, x, y, core, row)
    kv_own = arrange(jnp.stack([y, row]).astype(I32), pieces)
    kv_other = swap_core(kv_own)
    (o_far,), (l_far,) = attend(0, False, table, [far], kv_own, kv_other)
    o_far, l_far = shift_x(o_far, 2), shift_x(l_far, 2)
    (o_low, o_high), (l_low, l_high) = attend(2, False, table, [from_low, from_high], kv_own, kv_other)
    o_low, l_low = shift_x(o_low, -1), shift_x(l_low, -1)
    o_high, l_high = shift_x(o_high, 1), shift_x(l_high, 1)
    (o_own,), (l_own,) = attend(6, True, table, [queries], kv_own, kv_other)
    return combine([o_own, o_low, o_high, o_far], [l_own, l_low, l_high, l_far])


def solution(mesh):
    in_specs = (
        P("ctx", None, "row", None),
        P("ctx", None, "row", None),
        P("ctx", None, "row", None),
        P(),
    )
    out_specs = (P("ctx", None, "row", None), P("ctx", None, None, "row"))
    return jax.shard_map(local, mesh=mesh, in_specs=in_specs, out_specs=out_specs, check_vma=False)
```

```python
import functools
import itertools

import jax
import jax.numpy as jnp
from jax import lax
from jax.experimental import pallas as pl
from jax.experimental.pallas import tpu as pltpu
from jax.sharding import PartitionSpec as P

BF, F32, I32 = jnp.bfloat16, jnp.float32, jnp.int32
NX, NY, NC, NZ = 4, 4, 2, 4
HEADS, HD, SPAN = 8, 128, 384
ROWS = SPAN // NZ
HALF = ROWS // 2
TQ = HEADS * ROWS
NK = NY * NC * 2
MAX_STEPS = 8 * NK // 2 + 8
NEG = -1e30
SCALE = 1.4426950408889634 / HD**0.5
LN2 = 0.6931471805599453


def device(x, y, core, z):
    return ((x * NY + y) * NC + core) * NZ + z


def permute(a, target):
    places = itertools.product(range(NX), range(NY), range(NC), range(NZ))
    return lax.ppermute(a, ("ctx", "row"), [(device(*p), device(*target(*p))) for p in places])


def shift_x(a, d):
    return permute(a, lambda x, y, core, z: ((x + d) % NX, y, core, z))


def shift_plane(a, d, phase):
    def target(x, y, core, z):
        return (x, (y + d) % NY, core, z) if core == phase else (x, y, core, (z + d) % NZ)

    return permute(a, target)


def swap_core(a):
    return permute(a, lambda x, y, core, z: (x, y, 1 - core, z))


def dot_t(a, b):
    return lax.dot_general(a, b, (((1,), (1,)), ((), ())), preferred_element_type=F32)


def dot(a, b):
    return lax.dot_general(a, b, (((1,), (0,)), ((), ())), preferred_element_type=F32)


REL = (0, -1, 1, 2)


def gather_plane(a):
    line = jnp.stack([a, shift_plane(a, 1, 0), shift_plane(a, -1, 0), shift_plane(a, 2, 0)])
    low, high = shift_plane(line, 1, 1), shift_plane(line, -1, 1)
    return line, low, high


def gather_far(low, high):
    return shift_plane(low[:2], 1, 1), shift_plane(high[2:], -1, 1)


def place():
    ctx = lax.axis_index("ctx")
    return ctx // (NY * NC), ctx // NC % NY, ctx % NC, lax.axis_index("row")


def arrange_kernel(at, table, line, low, high, far_0, far_1, out_ref, vals):
    y, core, z = at[1], at[2], at[3]
    here_1, here_2 = jnp.where(core == 0, y, z), jnp.where(core == 0, z, y)
    for i, di in enumerate(REL):
        for j, dj in enumerate(REL):
            one, two = lax.rem(here_1 + di + 4, 4), lax.rem(here_2 + dj + 4, 4)
            span, part = jnp.where(core == 0, one, two) * 2, jnp.where(core == 0, two, one)
            at_row = pl.multiple_of(part * ROWS, 16)
            source = (line.at[i], low.at[i], high.at[i], (far_0, far_1)[i // 2].at[i % 2])[j]
            for slot in range(2):
                out_ref[span + slot, pl.ds(at_row, ROWS), :] = source[slot, :, :HD]
                vals[span + slot, pl.ds(at_row, ROWS), :] = source[slot, :, HD:]

    def turn(span, _):
        for b in range(3):
            block = vals[span, b * 128 : (b + 1) * 128, :]
            out_ref[span, SPAN + b * 128 : SPAN + (b + 1) * 128, :] = block.astype(F32).T.astype(BF)
        return 0

    lax.fori_loop(0, 2 * NY, turn, 0)


def arrange(at, table, parts):
    vmem = pl.BlockSpec(memory_space=pltpu.VMEM)
    return pl.pallas_call(
        arrange_kernel,
        out_shape=jax.ShapeDtypeStruct((2 * NY, 2 * SPAN, HD), BF),
        in_specs=[pl.BlockSpec(memory_space=pltpu.SMEM)] * 2 + [vmem] * 5,
        out_specs=vmem,
        scratch_shapes=[pltpu.VMEM((2 * NY, SPAN, HD), BF)],
        compiler_params=pltpu.CompilerParams(vmem_limit_bytes=40 << 20),
        name="arrange",
    )(at, table, *parts)


def attend_kernel(q0, slots, diagonal, table, *refs):
    nq, groups = len(slots), len(slots) // 2
    n_in = 1 + max(array for array, _ in slots)
    queries, (kv_own, kv_other), outs = refs[:n_in], refs[n_in : n_in + 2], refs[n_in + 2 : n_in + 2 + groups]
    kv, raw, qt, s0, s1, p0, p1, t0, t1, acc, ms, sems = refs[n_in + 2 + groups :]
    fetches = [
        pltpu.make_async_copy(queries[array].at[0, slot], raw.at[t], sems.at[2 + t])
        for t, (array, slot) in enumerate(slots)
    ]
    copies = [
        pltpu.make_async_copy(kv_own, kv.at[: NK // 2], sems.at[0]),
        pltpu.make_async_copy(kv_other, kv.at[NK // 2 :], sems.at[1]),
    ]
    for c in fetches + copies:
        c.start()
    for t in range(nq):
        fetches[t].wait()
        full = raw[t].astype(F32) * SCALE
        high = full.astype(BF)
        low = (full - high.astype(F32)).astype(BF)
        for h in range(HEADS):
            rows, cols = slice(h * ROWS, (h + 1) * ROWS), slice(h * HD, (h + 1) * HD)
            qt[t, rows, :HD] = high[:, cols]
            qt[t, rows, HD:] = low[:, cols]
    acc[...] = jnp.zeros_like(acc)
    ms[...] = jnp.full_like(ms, NEG)
    p1[...] = jnp.zeros_like(p1)
    base = table[6, q0]
    steps = table[6, q0 + nq] - base
    for c in copies:
        c.wait()

    def entry(row, i):
        return table[row, base + jnp.clip(i, 0, jnp.maximum(steps - 1, 0))]

    def tile_of(i):
        return jnp.where(jnp.logical_and(i >= 0, i < steps), entry(0, i) - q0, nq)

    def spans_of(i):
        return [jnp.clip(entry(1 + half, i), 0, NK - 1) for half in range(2)]

    def key_rows(i):
        k = jnp.concatenate([kv[k, :SPAN, :] for k in spans_of(i)], axis=0)
        return jnp.concatenate([k, k], axis=1)

    def value_rows(*spans):
        blocks = [kv[k, SPAN + b * HD : SPAN + (b + 1) * HD, :] for k in spans for b in range(3)]
        return jnp.concatenate([jnp.concatenate(blocks, axis=1), jnp.ones((16, SPAN * len(spans)), BF)], axis=0)

    def step(i, s_in, s_out, t_in, t_out, p_in, p_out, carry):
        m, rescale = carry
        first, pad = entry(3, i) == 1, entry(5, i) == 1
        m = jnp.where(first, NEG, m)
        new = jnp.maximum(jnp.maximum(m, t_in[0:1, :]), jnp.where(pad, NEG, t_in[1:2, :]))
        tops = (new, jnp.where(pad, -NEG, new))
        q = qt.at[jnp.clip(entry(0, i + 1) - q0, 0, nq - 1)]
        k = key_rows(i + 1)
        v = value_rows(*spans_of(i - 1))
        tile = tile_of(i - 1)
        for c in range(0, TQ, 256):
            cols = slice(c, c + 256)
            for half in range(2):
                rows = slice(half * SPAN, (half + 1) * SPAN)
                p_out[rows, cols] = jnp.exp2(s_in[rows, cols] - tops[half][:, cols]).astype(BF)
            acc[tile, :, cols] = acc[tile, :, cols] * rescale[:, cols] + dot(v, p_in[:, cols])
            x = dot_t(k, q[cols, :])
            s_out[:, cols] = x
            for half in range(2):
                t_out[half : half + 1, cols] = jnp.max(x[half * SPAN : (half + 1) * SPAN], axis=0, keepdims=True)
        ms[tile_of(i)] = new
        return new, jnp.exp2(m - new)

    def pair(ii, carry):
        i = 2 * ii
        carry = step(i, s0, s1, t0, t1, p1, p0, carry)
        return step(i + 1, s1, s0, t1, t0, p0, p1, carry)

    x = dot_t(key_rows(0), qt[jnp.clip(entry(0, 0) - q0, 0, nq - 1)])
    s0[...] = x
    for half in range(2):
        t0[half : half + 1, :] = jnp.max(x[half * SPAN : (half + 1) * SPAN], axis=0, keepdims=True)
    row = jnp.zeros((1, TQ), F32)
    pairs = (steps + 1) // 2
    m, rescale = lax.fori_loop(0, pairs, pair, (row + NEG, row + 1.0))
    i = 2 * pairs - 1
    tile = tile_of(i)
    acc[tile] = acc[tile] * rescale + dot(value_rows(*spans_of(i)), p1[...])
    if diagonal:
        key = lax.broadcasted_iota(I32, (SPAN, TQ), 0)
        query = lax.rem(lax.broadcasted_iota(I32, (SPAN, TQ), 1), ROWS) + table[6, 9] * ROWS
        seen = key <= query
        for slot, (s, p) in enumerate(((s0, p0), (s1, p1))):
            k = kv[table[6, 10] + slot, :SPAN, :]
            x = jnp.where(seen, dot_t(jnp.concatenate([k, k], axis=1), qt[slot]), NEG)
            s[:SPAN, :] = x
            new = jnp.maximum(ms[slot], jnp.max(x, axis=0, keepdims=True))
            rescale = jnp.exp2(ms[slot] - new)
            w = jnp.exp2(s[:SPAN, :] - new)
            ms[slot] = new
            v = value_rows(table[6, 10] + slot)
            acc[slot] = acc[slot] * rescale + dot(v, w.astype(BF))
    for g in range(groups):
        for slot in range(2):
            tile = 2 * g + slot
            total = acc[tile, HD : HD + 1, :]
            any_seen = total > 0.0
            safe = jnp.where(any_seen, total, 1.0)
            o = (acc[tile, :HD, :] * (1.0 / safe)).T.astype(BF)
            lse = jnp.where(any_seen, ms[tile] * LN2 + jnp.log(safe), NEG)
            for h in range(HEADS):
                rows = slice(h * ROWS, (h + 1) * ROWS)
                outs[g][slot, :ROWS, h * HD : (h + 1) * HD] = o[rows, :]
            logs = jnp.concatenate([lse[:, h * ROWS : (h + 1) * ROWS] for h in range(HEADS)] * 2, axis=0)
            for part in range(3):
                rounded = logs.astype(BF)
                outs[g][slot, ROWS:, part * HD : part * HD + ROWS] = rounded
                logs = logs - rounded.astype(F32)


def attend(q0, slots, diagonal, table, queries, kv_own, kv_other):
    groups = len(slots) // 2
    vmem = pl.BlockSpec(memory_space=pltpu.VMEM)
    hbm = pl.BlockSpec(memory_space=pl.ANY)
    tile = 2 * SPAN
    flops = 2 * groups * TQ * NK * SPAN * HD * 2
    return pl.pallas_call(
        functools.partial(attend_kernel, q0, slots, diagonal),
        out_shape=[jax.ShapeDtypeStruct((2, ROWS + 16, HEADS * HD), BF)] * groups,
        in_specs=[pl.BlockSpec(memory_space=pltpu.SMEM)] + [hbm] * (len(queries) + 2),
        out_specs=[vmem] * groups,
        scratch_shapes=[
            pltpu.VMEM((NK, 2 * SPAN, HD), BF),
            pltpu.VMEM((2 * groups, ROWS, HEADS * HD), BF),
            pltpu.VMEM((2 * groups, TQ, 2 * HD), BF),
            pltpu.VMEM((tile, TQ), F32),
            pltpu.VMEM((tile, TQ), F32),
            pltpu.VMEM((tile, TQ), BF),
            pltpu.VMEM((tile, TQ), BF),
            pltpu.VMEM((8, TQ), F32),
            pltpu.VMEM((8, TQ), F32),
            pltpu.VMEM((2 * groups + 1, HD + 16, TQ), F32),
            pltpu.VMEM((2 * groups + 1, 1, TQ), F32),
            pltpu.SemaphoreType.DMA((2 + 2 * groups,)),
        ],
        compiler_params=pltpu.CompilerParams(vmem_limit_bytes=26 << 20),
        cost_estimate=pl.CostEstimate(flops=flops, bytes_accessed=6 << 20, transcendentals=flops // 512),
        name="attend",
    )(table, *queries, kv_own, kv_other)


def combine_kernel(*refs):
    parts, (out_ref, lse_ref) = refs[:4], refs[4:]
    for slot in range(2):
        logs = [
            sum(r[slot, ROWS:, p * HD : p * HD + ROWS].astype(F32) for p in range(3))[:HEADS] for r in parts
        ]
        top = functools.reduce(jnp.maximum, logs)
        raw = [jnp.exp(v - top) for v in logs]
        total = sum(raw)
        lse_ref[0, slot] = top + jnp.log(total)
        shares = [(r / total).T for r in raw]
        for h in range(HEADS):
            cols = slice(h * HD, (h + 1) * HD)
            mixed = sum(s[:, h : h + 1] * r[slot, :ROWS, cols].astype(F32) for s, r in zip(shares, parts))
            out_ref[0, slot, :, cols] = mixed.astype(BF)


def combine(parts):
    vmem = pl.BlockSpec(memory_space=pltpu.VMEM)
    return pl.pallas_call(
        combine_kernel,
        out_shape=(
            jax.ShapeDtypeStruct((1, 2, ROWS, HEADS * HD), BF),
            jax.ShapeDtypeStruct((1, 2, HEADS, ROWS), F32),
        ),
        in_specs=[vmem] * 4,
        out_specs=(vmem, vmem),
        compiler_params=pltpu.CompilerParams(vmem_limit_bytes=32 << 20),
        name="combine",
    )(*parts)


ORDER = (2, -1, 1, 0)


def plan_kernel(at, assignment, table, order):
    x, y, core, row = at[0], at[1], at[2], at[3]
    keys = [
        assignment[(x * NY + i) * NC + c, slot] for c in (core, 1 - core) for i in range(NY) for slot in range(2)
    ]
    for i, key in enumerate(keys):
        order[sum((other < key).astype(I32) for other in keys)] = i
    begin = jnp.int32(0)
    for t in range(8):
        source = lax.rem(x + ORDER[t // 2] + NX, NX)
        query = assignment[(source * NY + y) * NC + core, t % 2]
        count = sum((key < query).astype(I32) for key in keys)
        tiles = lax.div(count + 1, 2)
        table[6, t] = begin

        def write(j, _):
            at_step = begin + j
            last = (j == tiles - 1).astype(I32)
            table[0, at_step] = t
            table[1, at_step] = order[2 * j]
            table[2, at_step] = order[2 * j + 1]
            table[3, at_step] = (j == 0).astype(I32)
            table[4, at_step] = last
            table[5, at_step] = last * lax.rem(count, 2)
            return 0

        lax.fori_loop(0, tiles, write, 0)
        begin = begin + tiles
    table[6, 8] = begin
    table[6, 9] = row
    table[6, 10] = y * 2


def plan(at, assignment):
    smem = pl.BlockSpec(memory_space=pltpu.SMEM)
    return pl.pallas_call(
        plan_kernel,
        out_shape=jax.ShapeDtypeStruct((8, MAX_STEPS), I32),
        in_specs=[smem, smem],
        out_specs=smem,
        scratch_shapes=[pltpu.SMEM((NK,), I32)],
        name="plan",
    )(at, assignment)


def local(queries, keys, values, assignment):
    at = jnp.stack(place()).astype(I32)
    line, low, high = gather_plane(jnp.concatenate([keys[0], values[0]], axis=-1))
    from_low, from_high = shift_x(queries, 1), shift_x(queries, -1)
    table = plan(at, assignment)
    low, high, from_low, from_high, table = lax.optimization_barrier((low, high, from_low, from_high, table))
    from_far = shift_x(from_low[:, :1], 1), shift_x(from_high[:, 1:], -1)
    parts = (line, low, high, *gather_far(low, high))
    *parts, from_far_0, from_far_1, table = lax.optimization_barrier((*parts, *from_far, table))
    from_far = from_far_0, from_far_1
    kv_own = arrange(at, table, parts)
    kv_other = swap_core(kv_own)
    kv = kv_own, kv_other
    both = ((0, 0), (0, 1))
    (far,) = attend(0, ((0, 0), (1, 0)), False, table, from_far, *kv)
    far = shift_x(far, 2)
    low, high = attend(2, both + ((1, 0), (1, 1)), False, table, (from_low, from_high), *kv)
    low, high = shift_x(low, -1), shift_x(high, 1)
    (own,) = attend(6, both, True, table, (queries,), *kv)
    return combine([own, low, high, far])


def solution(mesh):
    in_specs = (
        P("ctx", None, "row", None),
        P("ctx", None, "row", None),
        P("ctx", None, "row", None),
        P(),
    )
    out_specs = (P("ctx", None, "row", None), P("ctx", None, None, "row"))
    return jax.shard_map(local, mesh=mesh, in_specs=in_specs, out_specs=out_specs, check_vma=False)
```

```python
import functools
import itertools

import jax
import jax.numpy as jnp
from jax import lax
from jax.experimental import pallas as pl
from jax.experimental.pallas import tpu as pltpu
from jax.sharding import PartitionSpec as P

BF, F32, I32 = jnp.bfloat16, jnp.float32, jnp.int32
NX, NY, NC, NZ = 4, 4, 2, 4
HEADS, HD, SPAN = 8, 128, 384
ROWS = SPAN // NZ
HALF = ROWS // 2
TQ = HEADS * ROWS
NK = NY * NC * 2
MAX_STEPS = 8 * NK // 2 + 8
NEG = -1e30
MAX_RISE = 100.0
SCALE = 1.4426950408889634 / HD**0.5
LN2 = 0.6931471805599453


def device(x, y, core, z):
    return ((x * NY + y) * NC + core) * NZ + z


def permute(a, target):
    places = itertools.product(range(NX), range(NY), range(NC), range(NZ))
    return lax.ppermute(a, ("ctx", "row"), [(device(*p), device(*target(*p))) for p in places])


def shift_x(a, d):
    return permute(a, lambda x, y, core, z: ((x + d) % NX, y, core, z))


def shift_plane(a, d, phase):
    def target(x, y, core, z):
        return (x, (y + d) % NY, core, z) if core == phase else (x, y, core, (z + d) % NZ)

    return permute(a, target)


def swap_core(a):
    return permute(a, lambda x, y, core, z: (x, y, 1 - core, z))


def dot_t(a, b):
    return lax.dot_general(a, b, (((1,), (1,)), ((), ())), preferred_element_type=F32)


def dot(a, b):
    return lax.dot_general(a, b, (((1,), (0,)), ((), ())), preferred_element_type=F32)


REL = (0, -1, 1, 2)


def gather_plane(a):
    line = jnp.stack([a, shift_plane(a, 1, 0), shift_plane(a, -1, 0), shift_plane(a, 2, 0)])
    low, high = shift_plane(line, 1, 1), shift_plane(line, -1, 1)
    return line, low, high


def gather_far(low, high):
    return shift_plane(low[:2], 1, 1), shift_plane(high[2:], -1, 1)


def place():
    ctx = lax.axis_index("ctx")
    return ctx // (NY * NC), ctx // NC % NY, ctx % NC, lax.axis_index("row")


def arrange_kernel(at, table, line, low, high, far_0, far_1, out_ref, vals):
    y, core, z = at[1], at[2], at[3]
    here_1, here_2 = jnp.where(core == 0, y, z), jnp.where(core == 0, z, y)
    for i, di in enumerate(REL):
        for j, dj in enumerate(REL):
            one, two = lax.rem(here_1 + di + 4, 4), lax.rem(here_2 + dj + 4, 4)
            span, part = jnp.where(core == 0, one, two) * 2, jnp.where(core == 0, two, one)
            at_row = pl.multiple_of(part * ROWS, 16)
            source = (line.at[i], low.at[i], high.at[i], (far_0, far_1)[i // 2].at[i % 2])[j]
            for slot in range(2):
                out_ref[span + slot, pl.ds(at_row, ROWS), :] = source[slot, :, :HD]
                vals[span + slot, pl.ds(at_row, ROWS), :] = source[slot, :, HD:]

    def turn(span, _):
        for b in range(3):
            block = vals[span, b * 128 : (b + 1) * 128, :]
            out_ref[span, SPAN + b * 128 : SPAN + (b + 1) * 128, :] = block.astype(F32).T.astype(BF)
        return 0

    lax.fori_loop(0, 2 * NY, turn, 0)


def arrange(at, table, parts):
    vmem = pl.BlockSpec(memory_space=pltpu.VMEM)
    return pl.pallas_call(
        arrange_kernel,
        out_shape=jax.ShapeDtypeStruct((2 * NY, 2 * SPAN, HD), BF),
        in_specs=[pl.BlockSpec(memory_space=pltpu.SMEM)] * 2 + [vmem] * 5,
        out_specs=vmem,
        scratch_shapes=[pltpu.VMEM((2 * NY, SPAN, HD), BF)],
        compiler_params=pltpu.CompilerParams(vmem_limit_bytes=40 << 20),
        name="arrange",
    )(at, table, *parts)


def attend_kernel(q0, slots, diagonal, table, *refs):
    nq, groups = len(slots), len(slots) // 2
    n_in = 1 + max(array for array, _ in slots)
    queries, (kv_own, kv_other), outs = refs[:n_in], refs[n_in : n_in + 2], refs[n_in + 2 : n_in + 2 + groups]
    kv, raw, qt, s0, s1, p0, p1, t0, t1, acc, ms, starts, sems = refs[n_in + 2 + groups :]
    fetches = [
        pltpu.make_async_copy(queries[array].at[0, slot], raw.at[t], sems.at[2 + t])
        for t, (array, slot) in enumerate(slots)
    ]
    copies = [
        pltpu.make_async_copy(kv_own, kv.at[: NK // 2], sems.at[0]),
        pltpu.make_async_copy(kv_other, kv.at[NK // 2 :], sems.at[1]),
    ]
    for c in fetches + copies:
        c.start()
    for t in range(nq):
        fetches[t].wait()
        full = raw[t].astype(F32) * SCALE
        high = full.astype(BF)
        low = (full - high.astype(F32)).astype(BF)
        for h in range(HEADS):
            rows, cols = slice(h * ROWS, (h + 1) * ROWS), slice(h * HD, (h + 1) * HD)
            qt[t, rows, :HD] = high[:, cols]
            qt[t, rows, HD:] = low[:, cols]
    base = table[6, q0]
    steps = table[6, q0 + nq] - base
    for c in copies:
        c.wait()

    def entry(row, i):
        return table[row, base + jnp.clip(i, 0, jnp.maximum(steps - 1, 0))]

    def tile_of(i):
        return jnp.where(jnp.logical_and(i >= 0, i < steps), entry(0, i) - q0, nq)

    def spans_of(i):
        return [jnp.clip(entry(1 + half, i), 0, NK - 1) for half in range(2)]

    def key_rows(i):
        k = jnp.concatenate([kv[k, :SPAN, :] for k in spans_of(i)], axis=0)
        return jnp.concatenate([k, k], axis=1)

    def value_rows(*spans):
        blocks = [kv[k, SPAN + b * HD : SPAN + (b + 1) * HD, :] for k in spans for b in range(3)]
        return jnp.concatenate([jnp.concatenate(blocks, axis=1), jnp.ones((16, SPAN * len(spans)), BF)], axis=0)

    def query_tile(i):
        return jnp.clip(entry(0, i) - q0, 0, nq - 1)

    def clear():
        acc[...] = jnp.zeros_like(acc)
        ms[...] = jnp.full_like(ms, NEG)
        p1[...] = jnp.zeros_like(p1)

    def column_tops(x):
        return [jnp.max(x[half * SPAN : (half + 1) * SPAN], axis=0, keepdims=True) for half in range(2)]

    def last_product(rescale):
        i = 2 * pairs - 1
        tile = tile_of(i)
        acc[tile] = acc[tile] * rescale + dot(value_rows(*spans_of(i)), p1[...])

    def quick_step(i, p_in, p_out, carry):
        base_top, top, rescale, rise = carry
        first, pad = entry(3, i) == 1, entry(5, i) == 1
        ref = jnp.where(first, starts[query_tile(i)], top)
        tops = (ref, jnp.where(pad, -NEG, ref))
        q, k = qt.at[query_tile(i)], key_rows(i)
        v, tile = value_rows(*spans_of(i - 1)), tile_of(i - 1)
        seen = []
        for c in range(0, TQ, 256):
            cols = slice(c, c + 256)
            acc[tile, :, cols] = acc[tile, :, cols] * rescale[:, cols] + dot(v, p_in[:, cols])
            x = dot_t(k, q[cols, :])
            for half in range(2):
                rows = slice(half * SPAN, (half + 1) * SPAN)
                p_out[rows, cols] = jnp.exp2(x[rows] - tops[half][:, cols]).astype(BF)
            high, low = column_tops(x)
            seen.append(jnp.maximum(high, jnp.where(pad, NEG, low)))
        ms[tile_of(i)] = ref
        new = jnp.concatenate(seen, axis=1)
        rescale = jnp.where(first, 0.0, jnp.exp2(base_top - ref))
        return ref, jnp.maximum(ref, new), rescale, jnp.maximum(rise, new - ref)

    def quick_pair(ii, carry):
        carry = quick_step(2 * ii, p1, p0, carry)
        return quick_step(2 * ii + 1, p0, p1, carry)

    def safe_step(i, s_in, s_out, t_in, t_out, p_in, p_out, carry):
        m, rescale = carry
        first, pad = entry(3, i) == 1, entry(5, i) == 1
        m = jnp.where(first, NEG, m)
        new = jnp.maximum(jnp.maximum(m, t_in[0:1, :]), jnp.where(pad, NEG, t_in[1:2, :]))
        tops = (new, jnp.where(pad, -NEG, new))
        q, k = qt.at[query_tile(i + 1)], key_rows(i + 1)
        v, tile = value_rows(*spans_of(i - 1)), tile_of(i - 1)
        for c in range(0, TQ, 256):
            cols = slice(c, c + 256)
            for half in range(2):
                rows = slice(half * SPAN, (half + 1) * SPAN)
                p_out[rows, cols] = jnp.exp2(s_in[rows, cols] - tops[half][:, cols]).astype(BF)
            acc[tile, :, cols] = acc[tile, :, cols] * rescale[:, cols] + dot(v, p_in[:, cols])
            x = dot_t(k, q[cols, :])
            s_out[:, cols] = x
            t_out[0:1, cols], t_out[1:2, cols] = column_tops(x)
        ms[tile_of(i)] = new
        return new, jnp.exp2(m - new)

    def safe_pair(ii, carry):
        carry = safe_step(2 * ii, s0, s1, t0, t1, p1, p0, carry)
        return safe_step(2 * ii + 1, s1, s0, t1, t0, p0, p1, carry)

    row = jnp.zeros((1, TQ), F32)
    pairs = (steps + 1) // 2
    clear()
    for t in range(nq):
        k = kv[jnp.clip(table[1, table[6, q0 + t]], 0, NK - 1), :HD, :]
        x = dot_t(jnp.concatenate([k, k], axis=1), qt[t])
        starts[t] = jnp.max(x, axis=0, keepdims=True)
    _, _, rescale, rise = lax.fori_loop(0, pairs, quick_pair, (row, row, row, row))
    last_product(rescale)

    @pl.when(jnp.logical_not(jnp.max(rise) <= MAX_RISE))
    def _():
        clear()
        x = dot_t(key_rows(0), qt[query_tile(0)])
        s0[...] = x
        t0[0:1, :], t0[1:2, :] = column_tops(x)
        _, rescale = lax.fori_loop(0, pairs, safe_pair, (row + NEG, row + 1.0))
        last_product(rescale)

    if diagonal:
        key = lax.broadcasted_iota(I32, (SPAN, TQ), 0)
        query = lax.rem(lax.broadcasted_iota(I32, (SPAN, TQ), 1), ROWS) + table[6, 9] * ROWS
        seen = key <= query
        for slot, (s, p) in enumerate(((s0, p0), (s1, p1))):
            k = kv[table[6, 10] + slot, :SPAN, :]
            x = jnp.where(seen, dot_t(jnp.concatenate([k, k], axis=1), qt[slot]), NEG)
            s[:SPAN, :] = x
            new = jnp.maximum(ms[slot], jnp.max(x, axis=0, keepdims=True))
            rescale = jnp.exp2(ms[slot] - new)
            w = jnp.exp2(s[:SPAN, :] - new)
            ms[slot] = new
            v = value_rows(table[6, 10] + slot)
            acc[slot] = acc[slot] * rescale + dot(v, w.astype(BF))
    for g in range(groups):
        for slot in range(2):
            tile = 2 * g + slot
            total = acc[tile, HD : HD + 1, :]
            any_seen = total > 0.0
            safe = jnp.where(any_seen, total, 1.0)
            o = (acc[tile, :HD, :] * (1.0 / safe)).T.astype(BF)
            lse = jnp.where(any_seen, ms[tile] * LN2 + jnp.log(safe), NEG)
            for h in range(HEADS):
                rows = slice(h * ROWS, (h + 1) * ROWS)
                outs[g][slot, :ROWS, h * HD : (h + 1) * HD] = o[rows, :]
            logs = jnp.concatenate([lse[:, h * ROWS : (h + 1) * ROWS] for h in range(HEADS)] * 2, axis=0)
            for part in range(3):
                rounded = logs.astype(BF)
                outs[g][slot, ROWS:, part * HD : part * HD + ROWS] = rounded
                logs = logs - rounded.astype(F32)


def attend(q0, slots, diagonal, table, queries, kv_own, kv_other):
    groups = len(slots) // 2
    vmem = pl.BlockSpec(memory_space=pltpu.VMEM)
    hbm = pl.BlockSpec(memory_space=pl.ANY)
    tile = 2 * SPAN
    flops = 2 * groups * TQ * NK * SPAN * HD * 2
    return pl.pallas_call(
        functools.partial(attend_kernel, q0, slots, diagonal),
        out_shape=[jax.ShapeDtypeStruct((2, ROWS + 16, HEADS * HD), BF)] * groups,
        in_specs=[pl.BlockSpec(memory_space=pltpu.SMEM)] + [hbm] * (len(queries) + 2),
        out_specs=[vmem] * groups,
        scratch_shapes=[
            pltpu.VMEM((NK, 2 * SPAN, HD), BF),
            pltpu.VMEM((2 * groups, ROWS, HEADS * HD), BF),
            pltpu.VMEM((2 * groups, TQ, 2 * HD), BF),
            pltpu.VMEM((tile, TQ), F32),
            pltpu.VMEM((tile, TQ), F32),
            pltpu.VMEM((tile, TQ), BF),
            pltpu.VMEM((tile, TQ), BF),
            pltpu.VMEM((8, TQ), F32),
            pltpu.VMEM((8, TQ), F32),
            pltpu.VMEM((2 * groups + 1, HD + 16, TQ), F32),
            pltpu.VMEM((2 * groups + 1, 1, TQ), F32),
            pltpu.VMEM((2 * groups, 1, TQ), F32),
            pltpu.SemaphoreType.DMA((2 + 2 * groups,)),
        ],
        compiler_params=pltpu.CompilerParams(vmem_limit_bytes=26 << 20),
        cost_estimate=pl.CostEstimate(flops=flops, bytes_accessed=6 << 20, transcendentals=flops // 512),
        name="attend",
    )(table, *queries, kv_own, kv_other)


def combine_kernel(*refs):
    parts, (out_ref, lse_ref) = refs[:4], refs[4:]
    for slot in range(2):
        logs = [
            sum(r[slot, ROWS:, p * HD : p * HD + ROWS].astype(F32) for p in range(3))[:HEADS] for r in parts
        ]
        top = functools.reduce(jnp.maximum, logs)
        raw = [jnp.exp(v - top) for v in logs]
        total = sum(raw)
        lse_ref[0, slot] = top + jnp.log(total)
        shares = [(r / total).T for r in raw]
        for h in range(HEADS):
            cols = slice(h * HD, (h + 1) * HD)
            mixed = sum(s[:, h : h + 1] * r[slot, :ROWS, cols].astype(F32) for s, r in zip(shares, parts))
            out_ref[0, slot, :, cols] = mixed.astype(BF)


def combine(parts):
    vmem = pl.BlockSpec(memory_space=pltpu.VMEM)
    return pl.pallas_call(
        combine_kernel,
        out_shape=(
            jax.ShapeDtypeStruct((1, 2, ROWS, HEADS * HD), BF),
            jax.ShapeDtypeStruct((1, 2, HEADS, ROWS), F32),
        ),
        in_specs=[vmem] * 4,
        out_specs=(vmem, vmem),
        compiler_params=pltpu.CompilerParams(vmem_limit_bytes=32 << 20),
        name="combine",
    )(*parts)


ORDER = (2, -1, 1, 0)


def plan_kernel(at, assignment, table, order):
    x, y, core, row = at[0], at[1], at[2], at[3]
    keys = [
        assignment[(x * NY + i) * NC + c, slot] for c in (core, 1 - core) for i in range(NY) for slot in range(2)
    ]
    for i, key in enumerate(keys):
        order[sum((other < key).astype(I32) for other in keys)] = i
    begin = jnp.int32(0)
    for t in range(8):
        source = lax.rem(x + ORDER[t // 2] + NX, NX)
        query = assignment[(source * NY + y) * NC + core, t % 2]
        count = sum((key < query).astype(I32) for key in keys)
        tiles = lax.div(count + 1, 2)
        table[6, t] = begin

        def write(j, _):
            at_step = begin + j
            last = (j == tiles - 1).astype(I32)
            table[0, at_step] = t
            table[1, at_step] = order[2 * j]
            table[2, at_step] = order[2 * j + 1]
            table[3, at_step] = (j == 0).astype(I32)
            table[4, at_step] = last
            table[5, at_step] = last * lax.rem(count, 2)
            return 0

        lax.fori_loop(0, tiles, write, 0)
        begin = begin + tiles
    table[6, 8] = begin
    table[6, 9] = row
    table[6, 10] = y * 2


def plan(at, assignment):
    smem = pl.BlockSpec(memory_space=pltpu.SMEM)
    return pl.pallas_call(
        plan_kernel,
        out_shape=jax.ShapeDtypeStruct((8, MAX_STEPS), I32),
        in_specs=[smem, smem],
        out_specs=smem,
        scratch_shapes=[pltpu.SMEM((NK,), I32)],
        name="plan",
    )(at, assignment)


def local(queries, keys, values, assignment):
    at = jnp.stack(place()).astype(I32)
    line, low, high = gather_plane(jnp.concatenate([keys[0], values[0]], axis=-1))
    from_low, from_high = shift_x(queries, 1), shift_x(queries, -1)
    table = plan(at, assignment)
    low, high, from_low, from_high, table = lax.optimization_barrier((low, high, from_low, from_high, table))
    kv_own = arrange(at, table, (line, low, high, *gather_far(low, high)))
    kv_own, from_low, from_high = lax.optimization_barrier((kv_own, from_low, from_high))
    kv_other = swap_core(kv_own)
    from_far = shift_x(from_low[:, :1], 1), shift_x(from_high[:, 1:], -1)
    kv = kv_own, kv_other
    both = ((0, 0), (0, 1))
    (far,) = attend(0, ((0, 0), (1, 0)), False, table, from_far, *kv)
    far = shift_x(far, 2)
    low, high = attend(2, both + ((1, 0), (1, 1)), False, table, (from_low, from_high), *kv)
    low, high = shift_x(low, -1), shift_x(high, 1)
    (own,) = attend(6, both, True, table, (queries,), *kv)
    return combine([own, low, high, far])


def solution(mesh):
    in_specs = (
        P("ctx", None, "row", None),
        P("ctx", None, "row", None),
        P("ctx", None, "row", None),
        P(),
    )
    out_specs = (P("ctx", None, "row", None), P("ctx", None, None, "row"))
    return jax.shard_map(local, mesh=mesh, in_specs=in_specs, out_specs=out_specs, check_vma=False)
```

```python
import functools
import itertools

import jax
import jax.numpy as jnp
from jax import lax
from jax.experimental import pallas as pl
from jax.experimental.pallas import tpu as pltpu
from jax.sharding import PartitionSpec as P

BF, F32, I32 = jnp.bfloat16, jnp.float32, jnp.int32
NX, NY, NC, NZ = 4, 4, 2, 4
HEADS, HD, SPAN = 8, 128, 384
ROWS = SPAN // NZ
HALF = ROWS // 2
TQ = HEADS * ROWS
NK = NY * NC * 2
MAX_STEPS = 8 * NK // 2 + 8
NEG = -1e30
MAX_RISE = 100.0
SCALE = 1.4426950408889634 / HD**0.5
LN2 = 0.6931471805599453


def device(x, y, core, z):
    return ((x * NY + y) * NC + core) * NZ + z


def permute(a, target):
    places = itertools.product(range(NX), range(NY), range(NC), range(NZ))
    return lax.ppermute(a, ("ctx", "row"), [(device(*p), device(*target(*p))) for p in places])


def shift_x(a, d):
    return permute(a, lambda x, y, core, z: ((x + d) % NX, y, core, z))


def shift_plane(a, d, phase):
    def target(x, y, core, z):
        return (x, (y + d) % NY, core, z) if core == phase else (x, y, core, (z + d) % NZ)

    return permute(a, target)


def swap_core(a):
    return permute(a, lambda x, y, core, z: (x, y, 1 - core, z))


def dot_t(a, b):
    return lax.dot_general(a, b, (((1,), (1,)), ((), ())), preferred_element_type=F32)


def dot(a, b):
    return lax.dot_general(a, b, (((1,), (0,)), ((), ())), preferred_element_type=F32)


REL = (0, -1, 1, 2)


def gather_line(a):
    return jnp.stack([a, shift_plane(a, 1, 0), shift_plane(a, -1, 0), shift_plane(a, 2, 0)])


def gather_plane(line):
    return line, shift_plane(line, 1, 1), shift_plane(line, -1, 1)


def gather_far(low, high):
    return shift_plane(low[:2], 1, 1), shift_plane(high[2:], -1, 1)


def place():
    ctx = lax.axis_index("ctx")
    return ctx // (NY * NC), ctx // NC % NY, ctx % NC, lax.axis_index("row")


def arrange_kernel(at, table, line, low, high, far_0, far_1, out_ref, vals):
    y, core, z = at[1], at[2], at[3]
    here_1, here_2 = jnp.where(core == 0, y, z), jnp.where(core == 0, z, y)
    for i, di in enumerate(REL):
        for j, dj in enumerate(REL):
            one, two = lax.rem(here_1 + di + 4, 4), lax.rem(here_2 + dj + 4, 4)
            span, part = jnp.where(core == 0, one, two) * 2, jnp.where(core == 0, two, one)
            at_row = pl.multiple_of(part * ROWS, 16)
            source = (line.at[i], low.at[i], high.at[i], (far_0, far_1)[i // 2].at[i % 2])[j]
            for slot in range(2):
                out_ref[span + slot, pl.ds(at_row, ROWS), :] = source[slot, :, :HD]
                vals[span + slot, pl.ds(at_row, ROWS), :] = source[slot, :, HD:]

    def turn(span, _):
        for b in range(3):
            block = vals[span, b * 128 : (b + 1) * 128, :]
            out_ref[span, SPAN + b * 128 : SPAN + (b + 1) * 128, :] = block.astype(F32).T.astype(BF)
        return 0

    lax.fori_loop(0, 2 * NY, turn, 0)


def arrange(at, table, parts):
    vmem = pl.BlockSpec(memory_space=pltpu.VMEM)
    return pl.pallas_call(
        arrange_kernel,
        out_shape=jax.ShapeDtypeStruct((2 * NY, 2 * SPAN, HD), BF),
        in_specs=[pl.BlockSpec(memory_space=pltpu.SMEM)] * 2 + [vmem] * 5,
        out_specs=vmem,
        scratch_shapes=[pltpu.VMEM((2 * NY, SPAN, HD), BF)],
        compiler_params=pltpu.CompilerParams(vmem_limit_bytes=40 << 20),
        name="arrange",
    )(at, table, *parts)


def attend_kernel(q0, slots, diagonal, table, *refs):
    nq, groups = len(slots), len(slots) // 2
    n_in = 1 + max(array for array, _ in slots)
    queries, (kv_own, kv_other), outs = refs[:n_in], refs[n_in : n_in + 2], refs[n_in + 2 : n_in + 2 + groups]
    kv, raw, qt, s0, s1, p0, p1, t0, t1, acc, ms, starts, sems = refs[n_in + 2 + groups :]
    fetches = [
        pltpu.make_async_copy(queries[array].at[0, slot], raw.at[t], sems.at[2 + t])
        for t, (array, slot) in enumerate(slots)
    ]
    copies = [
        pltpu.make_async_copy(kv_own, kv.at[: NK // 2], sems.at[0]),
        pltpu.make_async_copy(kv_other, kv.at[NK // 2 :], sems.at[1]),
    ]
    for c in fetches + copies:
        c.start()
    for t in range(nq):
        fetches[t].wait()
        full = raw[t].astype(F32) * SCALE
        high = full.astype(BF)
        low = (full - high.astype(F32)).astype(BF)
        for h in range(HEADS):
            rows, cols = slice(h * ROWS, (h + 1) * ROWS), slice(h * HD, (h + 1) * HD)
            qt[t, rows, :HD] = high[:, cols]
            qt[t, rows, HD:] = low[:, cols]
    base = table[6, q0]
    steps = table[6, q0 + nq] - base
    for c in copies:
        c.wait()

    def entry(row, i):
        return table[row, base + jnp.clip(i, 0, jnp.maximum(steps - 1, 0))]

    def tile_of(i):
        return jnp.where(jnp.logical_and(i >= 0, i < steps), entry(0, i) - q0, nq)

    def spans_of(i):
        return [jnp.clip(entry(1 + half, i), 0, NK - 1) for half in range(2)]

    def key_rows(i):
        k = jnp.concatenate([kv[k, :SPAN, :] for k in spans_of(i)], axis=0)
        return jnp.concatenate([k, k], axis=1)

    def value_rows(*spans):
        blocks = [kv[k, SPAN + b * HD : SPAN + (b + 1) * HD, :] for k in spans for b in range(3)]
        return jnp.concatenate([jnp.concatenate(blocks, axis=1), jnp.ones((16, SPAN * len(spans)), BF)], axis=0)

    def query_tile(i):
        return jnp.clip(entry(0, i) - q0, 0, nq - 1)

    def clear():
        acc[...] = jnp.zeros_like(acc)
        ms[...] = jnp.full_like(ms, NEG)
        p1[...] = jnp.zeros_like(p1)

    def column_tops(x):
        return [jnp.max(x[half * SPAN : (half + 1) * SPAN], axis=0, keepdims=True) for half in range(2)]

    def last_product(i, p, rescale):
        tile = tile_of(i)
        acc[tile] = acc[tile] * rescale + dot(value_rows(*spans_of(i)), p[...])

    def quick_step(i, p_in, p_out, carry):
        base_top, top, rescale, rise = carry
        first, pad = entry(3, i) == 1, entry(5, i) == 1
        ref = jnp.where(first, starts[query_tile(i)], top)
        tops = (ref, jnp.where(pad, -NEG, ref))
        q, k = qt.at[query_tile(i)], key_rows(i)
        v, tile = value_rows(*spans_of(i - 1)), tile_of(i - 1)
        seen = []
        for c in range(0, TQ, 256):
            cols = slice(c, c + 256)
            acc[tile, :, cols] = acc[tile, :, cols] * rescale[:, cols] + dot(v, p_in[:, cols])
            x = dot_t(k, q[cols, :])
            for half in range(2):
                rows = slice(half * SPAN, (half + 1) * SPAN)
                p_out[rows, cols] = jnp.exp2(x[rows] - tops[half][:, cols]).astype(BF)
            high, low = column_tops(x)
            seen.append(jnp.maximum(high, jnp.where(pad, NEG, low)))
        ms[tile_of(i)] = ref
        new = jnp.concatenate(seen, axis=1)
        rescale = jnp.where(first, 0.0, jnp.exp2(base_top - ref))
        return ref, jnp.maximum(ref, new), rescale, jnp.maximum(rise, new - ref)

    def quick_pair(ii, carry):
        carry = quick_step(2 * ii, p1, p0, carry)
        return quick_step(2 * ii + 1, p0, p1, carry)

    def safe_step(i, s_in, s_out, t_in, t_out, p_in, p_out, carry):
        m, rescale = carry
        first, pad = entry(3, i) == 1, entry(5, i) == 1
        m = jnp.where(first, NEG, m)
        new = jnp.maximum(jnp.maximum(m, t_in[0:1, :]), jnp.where(pad, NEG, t_in[1:2, :]))
        tops = (new, jnp.where(pad, -NEG, new))
        q, k = qt.at[query_tile(i + 1)], key_rows(i + 1)
        v, tile = value_rows(*spans_of(i - 1)), tile_of(i - 1)
        for c in range(0, TQ, 256):
            cols = slice(c, c + 256)
            for half in range(2):
                rows = slice(half * SPAN, (half + 1) * SPAN)
                p_out[rows, cols] = jnp.exp2(s_in[rows, cols] - tops[half][:, cols]).astype(BF)
            acc[tile, :, cols] = acc[tile, :, cols] * rescale[:, cols] + dot(v, p_in[:, cols])
            x = dot_t(k, q[cols, :])
            s_out[:, cols] = x
            t_out[0:1, cols], t_out[1:2, cols] = column_tops(x)
        ms[tile_of(i)] = new
        return new, jnp.exp2(m - new)

    def safe_pair(ii, carry):
        carry = safe_step(2 * ii, s0, s1, t0, t1, p1, p0, carry)
        return safe_step(2 * ii + 1, s1, s0, t1, t0, p0, p1, carry)

    row = jnp.zeros((1, TQ), F32)
    pairs = (steps + 1) // 2
    clear()
    for t in range(nq):
        k = kv[jnp.clip(table[1, table[6, q0 + t]], 0, NK - 1), :HD, :]
        x = dot_t(jnp.concatenate([k, k], axis=1), qt[t])
        starts[t] = jnp.max(x, axis=0, keepdims=True)
    carry = lax.fori_loop(0, steps // 2, quick_pair, (row, row, row, row))

    def odd_end(carry):
        carry = quick_step(steps - 1, p1, p0, carry)
        last_product(steps - 1, p0, carry[2])
        return carry[3]

    def even_end(carry):
        last_product(steps - 1, p1, carry[2])
        return carry[3]

    rise = lax.cond(steps % 2 == 1, odd_end, even_end, carry)

    @pl.when(jnp.logical_not(jnp.max(rise) <= MAX_RISE))
    def _():
        clear()
        x = dot_t(key_rows(0), qt[query_tile(0)])
        s0[...] = x
        t0[0:1, :], t0[1:2, :] = column_tops(x)
        _, rescale = lax.fori_loop(0, pairs, safe_pair, (row + NEG, row + 1.0))
        last_product(2 * pairs - 1, p1, rescale)

    if diagonal:
        key = lax.broadcasted_iota(I32, (SPAN, TQ), 0)
        query = lax.rem(lax.broadcasted_iota(I32, (SPAN, TQ), 1), ROWS) + table[6, 9] * ROWS
        seen = key <= query
        for slot, (s, p) in enumerate(((s0, p0), (s1, p1))):
            k = kv[table[6, 10] + slot, :SPAN, :]
            x = jnp.where(seen, dot_t(jnp.concatenate([k, k], axis=1), qt[slot]), NEG)
            s[:SPAN, :] = x
            new = jnp.maximum(ms[slot], jnp.max(x, axis=0, keepdims=True))
            rescale = jnp.exp2(ms[slot] - new)
            w = jnp.exp2(s[:SPAN, :] - new)
            ms[slot] = new
            v = value_rows(table[6, 10] + slot)
            acc[slot] = acc[slot] * rescale + dot(v, w.astype(BF))
    for tile in range(nq):
        total = acc[tile, HD : HD + 1, :]
        any_seen = total > 0.0
        safe = jnp.where(any_seen, total, 1.0)
        out = outs[tile // 2]
        out[tile % 2, :HD, :] = (acc[tile, :HD, :] * (1.0 / safe)).astype(BF)
        left = jnp.broadcast_to(jnp.where(any_seen, ms[tile] * LN2 + jnp.log(safe), NEG), (16, TQ))
        for part in range(3):
            rounded = left.astype(BF)
            out[tile % 2, HD + 16 * part : HD + 16 * part + 16, :] = rounded
            left = left - rounded.astype(F32)


def attend(q0, slots, diagonal, table, queries, kv_own, kv_other):
    groups = len(slots) // 2
    vmem = pl.BlockSpec(memory_space=pltpu.VMEM)
    hbm = pl.BlockSpec(memory_space=pl.ANY)
    tile = 2 * SPAN
    flops = 2 * groups * TQ * NK * SPAN * HD * 2
    return pl.pallas_call(
        functools.partial(attend_kernel, q0, slots, diagonal),
        out_shape=[jax.ShapeDtypeStruct((2, HD + 48, TQ), BF)] * groups,
        in_specs=[pl.BlockSpec(memory_space=pltpu.SMEM)] + [hbm] * (len(queries) + 2),
        out_specs=[vmem] * groups,
        scratch_shapes=[
            pltpu.VMEM((NK, 2 * SPAN, HD), BF),
            pltpu.VMEM((2 * groups, ROWS, HEADS * HD), BF),
            pltpu.VMEM((2 * groups, TQ, 2 * HD), BF),
            pltpu.VMEM((tile, TQ), F32),
            pltpu.VMEM((tile, TQ), F32),
            pltpu.VMEM((tile, TQ), BF),
            pltpu.VMEM((tile, TQ), BF),
            pltpu.VMEM((8, TQ), F32),
            pltpu.VMEM((8, TQ), F32),
            pltpu.VMEM((2 * groups + 1, HD + 16, TQ), F32),
            pltpu.VMEM((2 * groups + 1, 1, TQ), F32),
            pltpu.VMEM((2 * groups, 1, TQ), F32),
            pltpu.SemaphoreType.DMA((2 + 2 * groups,)),
        ],
        compiler_params=pltpu.CompilerParams(vmem_limit_bytes=26 << 20),
        cost_estimate=pl.CostEstimate(flops=flops, bytes_accessed=6 << 20, transcendentals=flops // 512),
        name="attend",
    )(table, *queries, kv_own, kv_other)


def combine_kernel(*refs):
    parts, (out_ref, lse_ref) = refs[:4], refs[4:]
    for slot in range(2):
        logs = [sum(r[slot, HD + 16 * p : HD + 16 * p + 1, :].astype(F32) for p in range(3)) for r in parts]
        top = functools.reduce(jnp.maximum, logs)
        raw = [jnp.exp(v - top) for v in logs]
        total = sum(raw)
        lse = top + jnp.log(total)
        mixed = sum((w / total) * r[slot, :HD, :].astype(F32) for w, r in zip(raw, parts)).T
        for h in range(HEADS):
            rows = slice(h * ROWS, (h + 1) * ROWS)
            out_ref[0, slot, :, h * HD : (h + 1) * HD] = mixed[rows].astype(BF)
            lse_ref[0, slot, h : h + 1, :] = lse[:, rows]


def combine(parts):
    vmem = pl.BlockSpec(memory_space=pltpu.VMEM)
    return pl.pallas_call(
        combine_kernel,
        out_shape=(
            jax.ShapeDtypeStruct((1, 2, ROWS, HEADS * HD), BF),
            jax.ShapeDtypeStruct((1, 2, HEADS, ROWS), F32),
        ),
        in_specs=[vmem] * 4,
        out_specs=(vmem, vmem),
        compiler_params=pltpu.CompilerParams(vmem_limit_bytes=32 << 20),
        name="combine",
    )(*parts)


ORDER = (2, -1, 1, 0)


def plan_kernel(at, assignment, table, order):
    x, y, core, row = at[0], at[1], at[2], at[3]
    keys = [
        assignment[(x * NY + i) * NC + c, slot] for c in (core, 1 - core) for i in range(NY) for slot in range(2)
    ]
    for i, key in enumerate(keys):
        order[sum((other < key).astype(I32) for other in keys)] = i
    begin = jnp.int32(0)
    for t in range(8):
        source = lax.rem(x + ORDER[t // 2] + NX, NX)
        query = assignment[(source * NY + y) * NC + core, t % 2]
        count = sum((key < query).astype(I32) for key in keys)
        tiles = lax.div(count + 1, 2)
        table[6, t] = begin

        def write(j, _):
            at_step = begin + j
            last = (j == tiles - 1).astype(I32)
            table[0, at_step] = t
            table[1, at_step] = order[2 * j]
            table[2, at_step] = order[2 * j + 1]
            table[3, at_step] = (j == 0).astype(I32)
            table[4, at_step] = last
            table[5, at_step] = last * lax.rem(count, 2)
            return 0

        lax.fori_loop(0, tiles, write, 0)
        begin = begin + tiles
    table[6, 8] = begin
    table[6, 9] = row
    table[6, 10] = y * 2


def plan(at, assignment):
    smem = pl.BlockSpec(memory_space=pltpu.SMEM)
    return pl.pallas_call(
        plan_kernel,
        out_shape=jax.ShapeDtypeStruct((8, MAX_STEPS), I32),
        in_specs=[smem, smem],
        out_specs=smem,
        scratch_shapes=[pltpu.SMEM((NK,), I32)],
        name="plan",
    )(at, assignment)


def local(queries, keys, values, assignment):
    at = jnp.stack(place()).astype(I32)
    table = plan(at, assignment)
    near = gather_line(jnp.concatenate([keys[0], values[0]], axis=-1))
    near, queries_next = lax.optimization_barrier((near, queries))
    line, low, high = gather_plane(near)
    from_low, from_high = shift_x(queries_next, 1), shift_x(queries_next, -1)
    far = shift_plane(line, 2, 1)
    kv_own = arrange(at, table, (line, low, high, far[:2], far[2:]))
    kv_own, from_low, from_high = lax.optimization_barrier((kv_own, from_low, from_high))
    kv_other = swap_core(kv_own)
    from_far = shift_x(from_low[:, :1], 1), shift_x(from_high[:, 1:], -1)
    kv = kv_own, kv_other
    both = ((0, 0), (0, 1))
    (far,) = attend(0, ((0, 0), (1, 0)), False, table, from_far, *kv)
    far = shift_x(far, 2)
    low, high = attend(2, both + ((1, 0), (1, 1)), False, table, (from_low, from_high), *kv)
    low, high = shift_x(low, -1), shift_x(high, 1)
    (own,) = attend(6, both, True, table, (queries,), *kv)
    return combine([own, low, high, far])


def solution(mesh):
    in_specs = (
        P("ctx", None, "row", None),
        P("ctx", None, "row", None),
        P("ctx", None, "row", None),
        P(),
    )
    out_specs = (P("ctx", None, "row", None), P("ctx", None, None, "row"))
    return jax.shard_map(local, mesh=mesh, in_specs=in_specs, out_specs=out_specs, check_vma=False)
```

```python
import functools
import itertools

import jax
import jax.numpy as jnp
from jax import lax
from jax.experimental import pallas as pl
from jax.experimental.pallas import tpu as pltpu
from jax.sharding import PartitionSpec as P

BF, F32, I32 = jnp.bfloat16, jnp.float32, jnp.int32
NX, NY, NC, NZ = 4, 4, 2, 4
HEADS, HD, SPAN = 8, 128, 384
ROWS = SPAN // NZ
HALF = ROWS // 2
TQ = HEADS * ROWS
NK = NY * NC * 2
MAX_STEPS = 8 * NK // 2 + 8
NEG = -1e30
MAX_RISE = 100.0
SCALE = 1.4426950408889634 / HD**0.5
LN2 = 0.6931471805599453


def device(x, y, core, z):
    return ((x * NY + y) * NC + core) * NZ + z


def permute(a, target):
    places = itertools.product(range(NX), range(NY), range(NC), range(NZ))
    return lax.ppermute(a, ("ctx", "row"), [(device(*p), device(*target(*p))) for p in places])


def shift_x(a, d):
    return permute(a, lambda x, y, core, z: ((x + d) % NX, y, core, z))


def shift_plane(a, d, phase):
    def target(x, y, core, z):
        return (x, (y + d) % NY, core, z) if core == phase else (x, y, core, (z + d) % NZ)

    return permute(a, target)


def swap_core(a):
    return permute(a, lambda x, y, core, z: (x, y, 1 - core, z))


def dot_t(a, b):
    return lax.dot_general(a, b, (((1,), (1,)), ((), ())), preferred_element_type=F32)


def dot(a, b):
    return lax.dot_general(a, b, (((1,), (0,)), ((), ())), preferred_element_type=F32)


REL = (0, -1, 1, 2)


def gather_line(a):
    return jnp.stack([a, shift_plane(a, 1, 0), shift_plane(a, -1, 0), shift_plane(a, 2, 0)])


def gather_plane(line):
    return line, shift_plane(line, 1, 1), shift_plane(line, -1, 1)


def gather_far(low, high):
    return shift_plane(low[:2], 1, 1), shift_plane(high[2:], -1, 1)


def place():
    ctx = lax.axis_index("ctx")
    return ctx // (NY * NC), ctx // NC % NY, ctx % NC, lax.axis_index("row")


def arrange_kernel(line, low, high, far_0, far_1, out_ref, vals):
    _, y, core, z = place()
    here_1, here_2 = jnp.where(core == 0, y, z), jnp.where(core == 0, z, y)
    for i, di in enumerate(REL):
        for j, dj in enumerate(REL):
            one, two = lax.rem(here_1 + di + 4, 4), lax.rem(here_2 + dj + 4, 4)
            span, part = jnp.where(core == 0, one, two) * 2, jnp.where(core == 0, two, one)
            at_row = pl.multiple_of(part * ROWS, 16)
            source = (line.at[i], low.at[i], high.at[i], (far_0, far_1)[i // 2].at[i % 2])[j]
            for slot in range(2):
                out_ref[span + slot, pl.ds(at_row, ROWS), :] = source[slot, :, :HD]
                vals[span + slot, pl.ds(at_row, ROWS), :] = source[slot, :, HD:]

    def turn(span, _):
        for b in range(3):
            block = vals[span, b * 128 : (b + 1) * 128, :]
            out_ref[span, SPAN + b * 128 : SPAN + (b + 1) * 128, :] = block.astype(F32).T.astype(BF)
        return 0

    lax.fori_loop(0, 2 * NY, turn, 0)


def arrange(parts):
    vmem = pl.BlockSpec(memory_space=pltpu.VMEM)
    return pl.pallas_call(
        arrange_kernel,
        out_shape=jax.ShapeDtypeStruct((2 * NY, 2 * SPAN, HD), BF),
        in_specs=[vmem] * 5,
        out_specs=vmem,
        scratch_shapes=[pltpu.VMEM((2 * NY, SPAN, HD), BF)],
        compiler_params=pltpu.CompilerParams(vmem_limit_bytes=40 << 20),
        name="arrange",
    )(*parts)


def attend_kernel(q0, slots, diagonal, table, *refs):
    nq, groups = len(slots), len(slots) // 2
    n_in = 1 + max(array for array, _ in slots)
    queries, (kv_own, kv_other), outs = refs[:n_in], refs[n_in : n_in + 2], refs[n_in + 2 : n_in + 2 + groups]
    kv, raw, qt, s0, s1, p0, p1, t0, t1, acc, ms, starts, sems = refs[n_in + 2 + groups :]
    fetches = [
        pltpu.make_async_copy(queries[array].at[0, slot], raw.at[t], sems.at[2 + t])
        for t, (array, slot) in enumerate(slots)
    ]
    copies = [
        pltpu.make_async_copy(kv_own, kv.at[: NK // 2], sems.at[0]),
        pltpu.make_async_copy(kv_other, kv.at[NK // 2 :], sems.at[1]),
    ]
    for c in fetches + copies:
        c.start()
    for t in range(nq):
        fetches[t].wait()
        full = raw[t].astype(F32) * SCALE
        high = full.astype(BF)
        low = (full - high.astype(F32)).astype(BF)
        for h in range(HEADS):
            rows, cols = slice(h * ROWS, (h + 1) * ROWS), slice(h * HD, (h + 1) * HD)
            qt[t, rows, :HD] = high[:, cols]
            qt[t, rows, HD:] = low[:, cols]
    base = table[6, q0]
    steps = table[6, q0 + nq] - base
    for c in copies:
        c.wait()

    def entry(row, i):
        return table[row, base + jnp.clip(i, 0, jnp.maximum(steps - 1, 0))]

    def tile_of(i):
        return jnp.where(jnp.logical_and(i >= 0, i < steps), entry(0, i) - q0, nq)

    def spans_of(i):
        return [jnp.clip(entry(1 + half, i), 0, NK - 1) for half in range(2)]

    def key_rows(i):
        k = jnp.concatenate([kv[k, :SPAN, :] for k in spans_of(i)], axis=0)
        return jnp.concatenate([k, k], axis=1)

    def value_rows(*spans):
        blocks = [kv[k, SPAN + b * HD : SPAN + (b + 1) * HD, :] for k in spans for b in range(3)]
        return jnp.concatenate([jnp.concatenate(blocks, axis=1), jnp.ones((16, SPAN * len(spans)), BF)], axis=0)

    def query_tile(i):
        return jnp.clip(entry(0, i) - q0, 0, nq - 1)

    def clear():
        acc[...] = jnp.zeros_like(acc)
        ms[...] = jnp.full_like(ms, NEG)
        p1[...] = jnp.zeros_like(p1)

    def column_tops(x):
        return [jnp.max(x[half * SPAN : (half + 1) * SPAN], axis=0, keepdims=True) for half in range(2)]

    def last_product(i, p, rescale):
        tile = tile_of(i)
        acc[tile] = acc[tile] * rescale + dot(value_rows(*spans_of(i)), p[...])

    def quick_step(i, p_in, p_out, carry):
        base_top, top, rescale, rise = carry
        first, pad = entry(3, i) == 1, entry(5, i) == 1
        ref = jnp.where(first, starts[query_tile(i)], top)
        tops = (ref, jnp.where(pad, -NEG, ref))
        q, k = qt.at[query_tile(i)], key_rows(i)
        v, tile = value_rows(*spans_of(i - 1)), tile_of(i - 1)
        seen = []
        for c in range(0, TQ, 256):
            cols = slice(c, c + 256)
            acc[tile, :, cols] = acc[tile, :, cols] * rescale[:, cols] + dot(v, p_in[:, cols])
            x = dot_t(k, q[cols, :])
            for half in range(2):
                rows = slice(half * SPAN, (half + 1) * SPAN)
                p_out[rows, cols] = jnp.exp2(x[rows] - tops[half][:, cols]).astype(BF)
            high, low = column_tops(x)
            seen.append(jnp.maximum(high, jnp.where(pad, NEG, low)))
        ms[tile_of(i)] = ref
        new = jnp.concatenate(seen, axis=1)
        rescale = jnp.where(first, 0.0, jnp.exp2(base_top - ref))
        return ref, jnp.maximum(ref, new), rescale, jnp.maximum(rise, new - ref)

    def quick_pair(ii, carry):
        carry = quick_step(2 * ii, p1, p0, carry)
        return quick_step(2 * ii + 1, p0, p1, carry)

    def safe_step(i, s_in, s_out, t_in, t_out, p_in, p_out, carry):
        m, rescale = carry
        first, pad = entry(3, i) == 1, entry(5, i) == 1
        m = jnp.where(first, NEG, m)
        new = jnp.maximum(jnp.maximum(m, t_in[0:1, :]), jnp.where(pad, NEG, t_in[1:2, :]))
        tops = (new, jnp.where(pad, -NEG, new))
        q, k = qt.at[query_tile(i + 1)], key_rows(i + 1)
        v, tile = value_rows(*spans_of(i - 1)), tile_of(i - 1)
        for c in range(0, TQ, 256):
            cols = slice(c, c + 256)
            for half in range(2):
                rows = slice(half * SPAN, (half + 1) * SPAN)
                p_out[rows, cols] = jnp.exp2(s_in[rows, cols] - tops[half][:, cols]).astype(BF)
            acc[tile, :, cols] = acc[tile, :, cols] * rescale[:, cols] + dot(v, p_in[:, cols])
            x = dot_t(k, q[cols, :])
            s_out[:, cols] = x
            t_out[0:1, cols], t_out[1:2, cols] = column_tops(x)
        ms[tile_of(i)] = new
        return new, jnp.exp2(m - new)

    def safe_pair(ii, carry):
        carry = safe_step(2 * ii, s0, s1, t0, t1, p1, p0, carry)
        return safe_step(2 * ii + 1, s1, s0, t1, t0, p0, p1, carry)

    row = jnp.zeros((1, TQ), F32)
    pairs = (steps + 1) // 2
    clear()
    for t in range(nq):
        k = kv[jnp.clip(table[1, table[6, q0 + t]], 0, NK - 1), :HD, :]
        x = dot_t(jnp.concatenate([k, k], axis=1), qt[t])
        starts[t] = jnp.max(x, axis=0, keepdims=True)
    carry = lax.fori_loop(0, steps // 2, quick_pair, (row, row, row, row))

    def odd_end(carry):
        carry = quick_step(steps - 1, p1, p0, carry)
        last_product(steps - 1, p0, carry[2])
        return carry[3]

    def even_end(carry):
        last_product(steps - 1, p1, carry[2])
        return carry[3]

    rise = lax.cond(steps % 2 == 1, odd_end, even_end, carry)

    @pl.when(jnp.logical_not(jnp.max(rise) <= MAX_RISE))
    def _():
        clear()
        x = dot_t(key_rows(0), qt[query_tile(0)])
        s0[...] = x
        t0[0:1, :], t0[1:2, :] = column_tops(x)
        _, rescale = lax.fori_loop(0, pairs, safe_pair, (row + NEG, row + 1.0))
        last_product(2 * pairs - 1, p1, rescale)

    if diagonal:
        key = lax.broadcasted_iota(I32, (SPAN, TQ), 0)
        query = lax.rem(lax.broadcasted_iota(I32, (SPAN, TQ), 1), ROWS) + table[6, 9] * ROWS
        seen = key <= query
        for slot, (s, p) in enumerate(((s0, p0), (s1, p1))):
            k = kv[table[6, 10] + slot, :SPAN, :]
            x = jnp.where(seen, dot_t(jnp.concatenate([k, k], axis=1), qt[slot]), NEG)
            s[:SPAN, :] = x
            new = jnp.maximum(ms[slot], jnp.max(x, axis=0, keepdims=True))
            rescale = jnp.exp2(ms[slot] - new)
            w = jnp.exp2(s[:SPAN, :] - new)
            ms[slot] = new
            v = value_rows(table[6, 10] + slot)
            acc[slot] = acc[slot] * rescale + dot(v, w.astype(BF))
    for tile in range(nq):
        total = acc[tile, HD : HD + 1, :]
        any_seen = total > 0.0
        safe = jnp.where(any_seen, total, 1.0)
        out = outs[tile // 2]
        out[tile % 2, :HD, :] = (acc[tile, :HD, :] * (1.0 / safe)).astype(BF)
        left, rows = jnp.where(any_seen, ms[tile] * LN2 + jnp.log(safe), NEG), []
        for part in range(3):
            rows.append(left.astype(BF).astype(F32))
            left = left - rows[-1]
        out[tile % 2, HD:, :] = jnp.concatenate(rows + [jnp.zeros((13, TQ), F32)], axis=0).astype(BF)


def attend(q0, slots, diagonal, table, queries, kv_own, kv_other):
    groups = len(slots) // 2
    vmem = pl.BlockSpec(memory_space=pltpu.VMEM)
    hbm = pl.BlockSpec(memory_space=pl.ANY)
    tile = 2 * SPAN
    flops = 2 * groups * TQ * NK * SPAN * HD * 2
    return pl.pallas_call(
        functools.partial(attend_kernel, q0, slots, diagonal),
        out_shape=[jax.ShapeDtypeStruct((2, HD + 16, TQ), BF)] * groups,
        in_specs=[pl.BlockSpec(memory_space=pltpu.SMEM)] + [hbm] * (len(queries) + 2),
        out_specs=[vmem] * groups,
        scratch_shapes=[
            pltpu.VMEM((NK, 2 * SPAN, HD), BF),
            pltpu.VMEM((2 * groups, ROWS, HEADS * HD), BF),
            pltpu.VMEM((2 * groups, TQ, 2 * HD), BF),
            pltpu.VMEM((tile, TQ), F32),
            pltpu.VMEM((tile, TQ), F32),
            pltpu.VMEM((tile, TQ), BF),
            pltpu.VMEM((tile, TQ), BF),
            pltpu.VMEM((8, TQ), F32),
            pltpu.VMEM((8, TQ), F32),
            pltpu.VMEM((2 * groups + 1, HD + 16, TQ), F32),
            pltpu.VMEM((2 * groups + 1, 1, TQ), F32),
            pltpu.VMEM((2 * groups, 1, TQ), F32),
            pltpu.SemaphoreType.DMA((2 + 2 * groups,)),
        ],
        compiler_params=pltpu.CompilerParams(vmem_limit_bytes=26 << 20),
        cost_estimate=pl.CostEstimate(flops=flops, bytes_accessed=6 << 20, transcendentals=flops // 512),
        name="attend",
    )(table, *queries, kv_own, kv_other)


def combine_kernel(*refs):
    parts, (out_ref, lse_ref) = refs[:4], refs[4:]
    for slot in range(2):
        logs = [jnp.sum(r[slot, HD:, :].astype(F32), axis=0, keepdims=True) for r in parts]
        top = functools.reduce(jnp.maximum, logs)
        raw = [jnp.exp(v - top) for v in logs]
        total = sum(raw)
        lse = top + jnp.log(total)
        mixed = sum((w / total) * r[slot, :HD, :].astype(F32) for w, r in zip(raw, parts)).T
        for h in range(HEADS):
            rows = slice(h * ROWS, (h + 1) * ROWS)
            out_ref[0, slot, :, h * HD : (h + 1) * HD] = mixed[rows].astype(BF)
            lse_ref[0, slot, h : h + 1, :] = lse[:, rows]


def combine(parts):
    vmem = pl.BlockSpec(memory_space=pltpu.VMEM)
    return pl.pallas_call(
        combine_kernel,
        out_shape=(
            jax.ShapeDtypeStruct((1, 2, ROWS, HEADS * HD), BF),
            jax.ShapeDtypeStruct((1, 2, HEADS, ROWS), F32),
        ),
        in_specs=[vmem] * 4,
        out_specs=(vmem, vmem),
        compiler_params=pltpu.CompilerParams(vmem_limit_bytes=32 << 20),
        name="combine",
    )(*parts)


ORDER = (2, -1, 1, 0)


def plan_kernel(at, assignment, table, order):
    x, y, core, row = at[0], at[1], at[2], at[3]
    keys = [
        assignment[(x * NY + i) * NC + c, slot] for c in (core, 1 - core) for i in range(NY) for slot in range(2)
    ]
    for i, key in enumerate(keys):
        order[sum((other < key).astype(I32) for other in keys)] = i
    begin = jnp.int32(0)
    for t in range(8):
        source = lax.rem(x + ORDER[t // 2] + NX, NX)
        query = assignment[(source * NY + y) * NC + core, t % 2]
        count = sum((key < query).astype(I32) for key in keys)
        tiles = lax.div(count + 1, 2)
        table[6, t] = begin

        def write(j, _):
            at_step = begin + j
            last = (j == tiles - 1).astype(I32)
            table[0, at_step] = t
            table[1, at_step] = order[2 * j]
            table[2, at_step] = order[2 * j + 1]
            table[3, at_step] = (j == 0).astype(I32)
            table[4, at_step] = last
            table[5, at_step] = last * lax.rem(count, 2)
            return 0

        lax.fori_loop(0, tiles, write, 0)
        begin = begin + tiles
    table[6, 8] = begin
    table[6, 9] = row
    table[6, 10] = y * 2


def plan(at, assignment):
    smem = pl.BlockSpec(memory_space=pltpu.SMEM)
    return pl.pallas_call(
        plan_kernel,
        out_shape=jax.ShapeDtypeStruct((8, MAX_STEPS), I32),
        in_specs=[smem, smem],
        out_specs=smem,
        scratch_shapes=[pltpu.SMEM((NK,), I32)],
        name="plan",
    )(at, assignment)


def local(queries, keys, values, assignment):
    at = jnp.stack(place()).astype(I32)
    table = plan(at, assignment)
    near = gather_line(jnp.concatenate([keys[0], values[0]], axis=-1))
    near, queries_next = lax.optimization_barrier((near, queries))
    line, low, high = gather_plane(near)
    from_low, from_high = shift_x(queries_next, 1), shift_x(queries_next, -1)
    far = shift_plane(line, 2, 1)
    low, high, far, table = lax.optimization_barrier((low, high, far, table))
    kv_own = arrange((line, low, high, far[:2], far[2:]))
    kv_own, from_low, from_high = lax.optimization_barrier((kv_own, from_low, from_high))
    kv_other = swap_core(kv_own)
    from_far = shift_x(from_low[:, :1], 1), shift_x(from_high[:, 1:], -1)
    kv = kv_own, kv_other
    both = ((0, 0), (0, 1))
    (far,) = attend(0, ((0, 0), (1, 0)), False, table, from_far, *kv)
    far = shift_x(far, 2)
    low, high = attend(2, both + ((1, 0), (1, 1)), False, table, (from_low, from_high), *kv)
    low, high = shift_x(low, -1), shift_x(high, 1)
    (own,) = attend(6, both, True, table, (queries,), *kv)
    return combine([own, low, high, far])


def solution(mesh):
    in_specs = (
        P("ctx", None, "row", None),
        P("ctx", None, "row", None),
        P("ctx", None, "row", None),
        P(),
    )
    out_specs = (P("ctx", None, "row", None), P("ctx", None, None, "row"))
    return jax.shard_map(local, mesh=mesh, in_specs=in_specs, out_specs=out_specs, check_vma=False)
```

```python
import functools
import itertools

import jax
import jax.numpy as jnp
from jax import lax
from jax.experimental import pallas as pl
from jax.experimental.pallas import tpu as pltpu
from jax.sharding import PartitionSpec as P

BF, F32, I32 = jnp.bfloat16, jnp.float32, jnp.int32
NX, NY, NC, NZ = 4, 4, 2, 4
HEADS, HD, SPAN = 8, 128, 384
ROWS = SPAN // NZ
HALF = ROWS // 2
TQ = HEADS * ROWS
NK = NY * NC * 2
MAX_STEPS = 8 * NK // 2 + 8
NEG = -1e30
MAX_RISE = 100.0
SCALE = 1.4426950408889634 / HD**0.5
LN2 = 0.6931471805599453


def device(x, y, core, z):
    return ((x * NY + y) * NC + core) * NZ + z


def permute(a, target):
    places = itertools.product(range(NX), range(NY), range(NC), range(NZ))
    return lax.ppermute(a, ("ctx", "row"), [(device(*p), device(*target(*p))) for p in places])


def shift_x(a, d):
    return permute(a, lambda x, y, core, z: ((x + d) % NX, y, core, z))


def shift_plane(a, d, phase):
    def target(x, y, core, z):
        return (x, (y + d) % NY, core, z) if core == phase else (x, y, core, (z + d) % NZ)

    return permute(a, target)


def swap_core(a):
    return permute(a, lambda x, y, core, z: (x, y, 1 - core, z))


def dot_t(a, b):
    return lax.dot_general(a, b, (((1,), (1,)), ((), ())), preferred_element_type=F32)


def dot(a, b):
    return lax.dot_general(a, b, (((1,), (0,)), ((), ())), preferred_element_type=F32)


REL = (0, -1, 1, 2)


def gather_line(a):
    return jnp.stack([a, shift_plane(a, 1, 0), shift_plane(a, -1, 0), shift_plane(a, 2, 0)])


def gather_plane(line):
    return line, shift_plane(line, 1, 1), shift_plane(line, -1, 1)


def gather_far(low, high):
    return shift_plane(low[:2], 1, 1), shift_plane(high[2:], -1, 1)


def place():
    ctx = lax.axis_index("ctx")
    return ctx // (NY * NC), ctx // NC % NY, ctx % NC, lax.axis_index("row")


def arrange_kernel(line, low, high, far_0, far_1, out_ref, vals):
    _, y, core, z = place()
    here_1, here_2 = jnp.where(core == 0, y, z), jnp.where(core == 0, z, y)
    for i, di in enumerate(REL):
        for j, dj in enumerate(REL):
            one, two = lax.rem(here_1 + di + 4, 4), lax.rem(here_2 + dj + 4, 4)
            span, part = jnp.where(core == 0, one, two) * 2, jnp.where(core == 0, two, one)
            at_row = pl.multiple_of(part * ROWS, 16)
            source = (line.at[i], low.at[i], high.at[i], (far_0, far_1)[i // 2].at[i % 2])[j]
            for slot in range(2):
                out_ref[span + slot, pl.ds(at_row, ROWS), :] = source[slot, :, :HD]
                vals[span + slot, pl.ds(at_row, ROWS), :] = source[slot, :, HD:]

    def turn(span, _):
        for b in range(3):
            block = vals[span, b * 128 : (b + 1) * 128, :]
            out_ref[span, SPAN + b * 128 : SPAN + (b + 1) * 128, :] = block.astype(F32).T.astype(BF)
        return 0

    lax.fori_loop(0, 2 * NY, turn, 0)


def arrange(parts):
    vmem = pl.BlockSpec(memory_space=pltpu.VMEM)
    return pl.pallas_call(
        arrange_kernel,
        out_shape=jax.ShapeDtypeStruct((2 * NY, 2 * SPAN, HD), BF),
        in_specs=[vmem] * 5,
        out_specs=vmem,
        scratch_shapes=[pltpu.VMEM((2 * NY, SPAN, HD), BF)],
        compiler_params=pltpu.CompilerParams(vmem_limit_bytes=40 << 20),
        name="arrange",
    )(*parts)


def attend_kernel(q0, slots, diagonal, table, *refs):
    nq, groups = len(slots), len(slots) // 2
    n_in = 1 + max(array for array, _ in slots)
    queries, (kv_own, kv_other), outs = refs[:n_in], refs[n_in : n_in + 2], refs[n_in + 2 : n_in + 2 + groups]
    kv, raw, qt, s0, s1, p0, p1, t0, t1, acc, ms, starts, sems = refs[n_in + 2 + groups :]
    fetches = [
        pltpu.make_async_copy(queries[array].at[0, slot], raw.at[t], sems.at[2 + t])
        for t, (array, slot) in enumerate(slots)
    ]
    copies = [
        pltpu.make_async_copy(kv_own, kv.at[: NK // 2], sems.at[0]),
        pltpu.make_async_copy(kv_other, kv.at[NK // 2 :], sems.at[1]),
    ]
    for c in fetches + copies:
        c.start()
    def clear():
        acc[...] = jnp.zeros_like(acc)
        ms[...] = jnp.full_like(ms, NEG)
        p1[...] = jnp.zeros_like(p1)

    clear()
    for t in range(nq):
        fetches[t].wait()
        full = raw[t].astype(F32) * SCALE
        high = full.astype(BF)
        low = (full - high.astype(F32)).astype(BF)
        for h in range(HEADS):
            rows, cols = slice(h * ROWS, (h + 1) * ROWS), slice(h * HD, (h + 1) * HD)
            qt[t, rows, :HD] = high[:, cols]
            qt[t, rows, HD:] = low[:, cols]
    base = table[6, q0]
    steps = table[6, q0 + nq] - base
    for c in copies:
        c.wait()

    def entry(row, i):
        return table[row, base + jnp.clip(i, 0, jnp.maximum(steps - 1, 0))]

    def tile_of(i):
        return jnp.where(jnp.logical_and(i >= 0, i < steps), entry(0, i) - q0, nq)

    def spans_of(i):
        return [jnp.clip(entry(1 + half, i), 0, NK - 1) for half in range(2)]

    def key_rows(i):
        k = jnp.concatenate([kv[k, :SPAN, :] for k in spans_of(i)], axis=0)
        return jnp.concatenate([k, k], axis=1)

    def value_rows(*spans):
        blocks = [kv[k, SPAN + b * HD : SPAN + (b + 1) * HD, :] for k in spans for b in range(3)]
        return jnp.concatenate([jnp.concatenate(blocks, axis=1), jnp.ones((16, SPAN * len(spans)), BF)], axis=0)

    def query_tile(i):
        return jnp.clip(entry(0, i) - q0, 0, nq - 1)

    def column_tops(x):
        return [jnp.max(x[half * SPAN : (half + 1) * SPAN], axis=0, keepdims=True) for half in range(2)]

    def last_product(i, p, rescale):
        tile = tile_of(i)
        acc[tile] = acc[tile] * rescale + dot(value_rows(*spans_of(i)), p[...])

    def quick_step(i, p_in, p_out, carry):
        base_top, top, rescale, rise = carry
        first, pad = entry(3, i) == 1, entry(5, i) == 1
        ref = jnp.where(first, starts[query_tile(i)], top)
        tops = (ref, jnp.where(pad, -NEG, ref))
        q, k = qt.at[query_tile(i)], key_rows(i)
        v, tile = value_rows(*spans_of(i - 1)), tile_of(i - 1)
        seen = []
        for c in range(0, TQ, 256):
            cols = slice(c, c + 256)
            acc[tile, :, cols] = acc[tile, :, cols] * rescale[:, cols] + dot(v, p_in[:, cols])
            x = dot_t(k, q[cols, :])
            for half in range(2):
                rows = slice(half * SPAN, (half + 1) * SPAN)
                p_out[rows, cols] = jnp.exp2(x[rows] - tops[half][:, cols]).astype(BF)
            high, low = column_tops(x)
            seen.append(jnp.maximum(high, jnp.where(pad, NEG, low)))
        ms[tile_of(i)] = ref
        new = jnp.concatenate(seen, axis=1)
        rescale = jnp.where(first, 0.0, jnp.exp2(base_top - ref))
        return ref, jnp.maximum(ref, new), rescale, jnp.maximum(rise, new - ref)

    def quick_pair(ii, carry):
        carry = quick_step(2 * ii, p1, p0, carry)
        return quick_step(2 * ii + 1, p0, p1, carry)

    def safe_step(i, s_in, s_out, t_in, t_out, p_in, p_out, carry):
        m, rescale = carry
        first, pad = entry(3, i) == 1, entry(5, i) == 1
        m = jnp.where(first, NEG, m)
        new = jnp.maximum(jnp.maximum(m, t_in[0:1, :]), jnp.where(pad, NEG, t_in[1:2, :]))
        tops = (new, jnp.where(pad, -NEG, new))
        q, k = qt.at[query_tile(i + 1)], key_rows(i + 1)
        v, tile = value_rows(*spans_of(i - 1)), tile_of(i - 1)
        for c in range(0, TQ, 256):
            cols = slice(c, c + 256)
            for half in range(2):
                rows = slice(half * SPAN, (half + 1) * SPAN)
                p_out[rows, cols] = jnp.exp2(s_in[rows, cols] - tops[half][:, cols]).astype(BF)
            acc[tile, :, cols] = acc[tile, :, cols] * rescale[:, cols] + dot(v, p_in[:, cols])
            x = dot_t(k, q[cols, :])
            s_out[:, cols] = x
            t_out[0:1, cols], t_out[1:2, cols] = column_tops(x)
        ms[tile_of(i)] = new
        return new, jnp.exp2(m - new)

    def safe_pair(ii, carry):
        carry = safe_step(2 * ii, s0, s1, t0, t1, p1, p0, carry)
        return safe_step(2 * ii + 1, s1, s0, t1, t0, p0, p1, carry)

    row = jnp.zeros((1, TQ), F32)
    pairs = (steps + 1) // 2
    for t in range(nq):
        k = kv[jnp.clip(table[1, table[6, q0 + t]], 0, NK - 1), :HD, :]
        x = dot_t(jnp.concatenate([k, k], axis=1), qt[t])
        starts[t] = jnp.max(x, axis=0, keepdims=True)
    carry = lax.fori_loop(0, steps // 2, quick_pair, (row, row, row, row))

    def odd_end(carry):
        carry = quick_step(steps - 1, p1, p0, carry)
        last_product(steps - 1, p0, carry[2])
        return carry[3]

    def even_end(carry):
        last_product(steps - 1, p1, carry[2])
        return carry[3]

    rise = lax.cond(steps % 2 == 1, odd_end, even_end, carry)

    @pl.when(jnp.logical_not(jnp.max(rise) <= MAX_RISE))
    def _():
        clear()
        x = dot_t(key_rows(0), qt[query_tile(0)])
        s0[...] = x
        t0[0:1, :], t0[1:2, :] = column_tops(x)
        _, rescale = lax.fori_loop(0, pairs, safe_pair, (row + NEG, row + 1.0))
        last_product(2 * pairs - 1, p1, rescale)

    if diagonal:
        key = lax.broadcasted_iota(I32, (SPAN, TQ), 0)
        query = lax.rem(lax.broadcasted_iota(I32, (SPAN, TQ), 1), ROWS) + table[6, 9] * ROWS
        seen = key <= query
        for slot, (s, p) in enumerate(((s0, p0), (s1, p1))):
            k = kv[table[6, 10] + slot, :SPAN, :]
            x = jnp.where(seen, dot_t(jnp.concatenate([k, k], axis=1), qt[slot]), NEG)
            s[:SPAN, :] = x
            new = jnp.maximum(ms[slot], jnp.max(x, axis=0, keepdims=True))
            rescale = jnp.exp2(ms[slot] - new)
            w = jnp.exp2(s[:SPAN, :] - new)
            ms[slot] = new
            v = value_rows(table[6, 10] + slot)
            acc[slot] = acc[slot] * rescale + dot(v, w.astype(BF))
    for tile in range(nq):
        total = acc[tile, HD : HD + 1, :]
        any_seen = total > 0.0
        safe = jnp.where(any_seen, total, 1.0)
        out = outs[tile // 2]
        out[tile % 2, :HD, :] = (acc[tile, :HD, :] * (1.0 / safe)).astype(BF)
        left, rows = jnp.where(any_seen, ms[tile] * LN2 + jnp.log(safe), NEG), []
        for part in range(3):
            rows.append(left.astype(BF).astype(F32))
            left = left - rows[-1]
        out[tile % 2, HD:, :] = jnp.concatenate(rows + [jnp.zeros((13, TQ), F32)], axis=0).astype(BF)


def attend(q0, slots, diagonal, table, queries, kv_own, kv_other):
    groups = len(slots) // 2
    vmem = pl.BlockSpec(memory_space=pltpu.VMEM)
    hbm = pl.BlockSpec(memory_space=pl.ANY)
    tile = 2 * SPAN
    flops = 2 * groups * TQ * NK * SPAN * HD * 2
    return pl.pallas_call(
        functools.partial(attend_kernel, q0, slots, diagonal),
        out_shape=[jax.ShapeDtypeStruct((2, HD + 16, TQ), BF)] * groups,
        in_specs=[pl.BlockSpec(memory_space=pltpu.SMEM)] + [hbm] * (len(queries) + 2),
        out_specs=[vmem] * groups,
        scratch_shapes=[
            pltpu.VMEM((NK, 2 * SPAN, HD), BF),
            pltpu.VMEM((2 * groups, ROWS, HEADS * HD), BF),
            pltpu.VMEM((2 * groups, TQ, 2 * HD), BF),
            pltpu.VMEM((tile, TQ), F32),
            pltpu.VMEM((tile, TQ), F32),
            pltpu.VMEM((tile, TQ), BF),
            pltpu.VMEM((tile, TQ), BF),
            pltpu.VMEM((8, TQ), F32),
            pltpu.VMEM((8, TQ), F32),
            pltpu.VMEM((2 * groups + 1, HD + 16, TQ), F32),
            pltpu.VMEM((2 * groups + 1, 1, TQ), F32),
            pltpu.VMEM((2 * groups, 1, TQ), F32),
            pltpu.SemaphoreType.DMA((2 + 2 * groups,)),
        ],
        compiler_params=pltpu.CompilerParams(vmem_limit_bytes=26 << 20),
        cost_estimate=pl.CostEstimate(flops=flops, bytes_accessed=6 << 20, transcendentals=flops // 512),
        name="attend",
    )(table, *queries, kv_own, kv_other)


def combine_kernel(*refs):
    parts, (out_ref, lse_ref) = refs[:4], refs[4:]
    for slot in range(2):
        logs = [jnp.sum(r[slot, HD:, :].astype(F32), axis=0, keepdims=True) for r in parts]
        top = functools.reduce(jnp.maximum, logs)
        raw = [jnp.exp(v - top) for v in logs]
        total = sum(raw)
        lse = top + jnp.log(total)
        mixed = sum((w / total) * r[slot, :HD, :].astype(F32) for w, r in zip(raw, parts)).T
        for h in range(HEADS):
            rows = slice(h * ROWS, (h + 1) * ROWS)
            out_ref[0, slot, :, h * HD : (h + 1) * HD] = mixed[rows].astype(BF)
            lse_ref[0, slot, h : h + 1, :] = lse[:, rows]


def combine(parts):
    vmem = pl.BlockSpec(memory_space=pltpu.VMEM)
    return pl.pallas_call(
        combine_kernel,
        out_shape=(
            jax.ShapeDtypeStruct((1, 2, ROWS, HEADS * HD), BF),
            jax.ShapeDtypeStruct((1, 2, HEADS, ROWS), F32),
        ),
        in_specs=[vmem] * 4,
        out_specs=(vmem, vmem),
        compiler_params=pltpu.CompilerParams(vmem_limit_bytes=32 << 20),
        name="combine",
    )(*parts)


ORDER = (2, -1, 1, 0)


def plan_kernel(assignment, table, order):
    x, y, core, row = place()
    keys = [
        assignment[(x * NY + i) * NC + c, slot] for c in (core, 1 - core) for i in range(NY) for slot in range(2)
    ]
    for i, key in enumerate(keys):
        order[sum((other < key).astype(I32) for other in keys)] = i
    begin = jnp.int32(0)
    for t in range(8):
        source = lax.rem(x + ORDER[t // 2] + NX, NX)
        query = assignment[(source * NY + y) * NC + core, t % 2]
        count = sum((key < query).astype(I32) for key in keys)
        tiles = lax.div(count + 1, 2)
        table[6, t] = begin

        def write(j, _):
            at_step = begin + j
            last = (j == tiles - 1).astype(I32)
            table[0, at_step] = t
            table[1, at_step] = order[2 * j]
            table[2, at_step] = order[2 * j + 1]
            table[3, at_step] = (j == 0).astype(I32)
            table[4, at_step] = last
            table[5, at_step] = last * lax.rem(count, 2)
            return 0

        lax.fori_loop(0, tiles, write, 0)
        begin = begin + tiles
    table[6, 8] = begin
    table[6, 9] = row
    table[6, 10] = y * 2


def plan(assignment):
    smem = pl.BlockSpec(memory_space=pltpu.SMEM)
    return pl.pallas_call(
        plan_kernel,
        out_shape=jax.ShapeDtypeStruct((8, MAX_STEPS), I32),
        in_specs=[smem],
        out_specs=smem,
        scratch_shapes=[pltpu.SMEM((NK,), I32)],
        name="plan",
    )(assignment)


def local(queries, keys, values, assignment):
    table = plan(assignment)
    near = gather_line(jnp.concatenate([keys[0], values[0]], axis=-1))
    near, queries_next = lax.optimization_barrier((near, queries))
    line, low, high = gather_plane(near)
    from_low, from_high = shift_x(queries_next, 1), shift_x(queries_next, -1)
    far = shift_plane(line, 2, 1)
    low, high, far, table = lax.optimization_barrier((low, high, far, table))
    kv_own = arrange((line, low, high, far[:2], far[2:]))
    kv_own, from_low, from_high = lax.optimization_barrier((kv_own, from_low, from_high))
    kv_other = swap_core(kv_own)
    from_far = shift_x(from_low[:, :1], 1), shift_x(from_high[:, 1:], -1)
    kv = kv_own, kv_other
    both = ((0, 0), (0, 1))
    (far,) = attend(0, ((0, 0), (1, 0)), False, table, from_far, *kv)
    far = shift_x(far, 2)
    low, high = attend(2, both + ((1, 0), (1, 1)), False, table, (from_low, from_high), *kv)
    low, high = shift_x(low, -1), shift_x(high, 1)
    (own,) = attend(6, both, True, table, (queries,), *kv)
    return combine([own, low, high, far])


def solution(mesh):
    in_specs = (
        P("ctx", None, "row", None),
        P("ctx", None, "row", None),
        P("ctx", None, "row", None),
        P(),
    )
    out_specs = (P("ctx", None, "row", None), P("ctx", None, None, "row"))
    return jax.shard_map(local, mesh=mesh, in_specs=in_specs, out_specs=out_specs, check_vma=False)
```
